128 devices in a mesh: rows: 8 (over y, core), cols: 16 (over z, x).
Axes of the slice: x: 4, y: 4, z: 4, core: 2. Of those that a mesh axis runs over, the one named last changes fastest.
Arguments:
- state: float32 [8, 256, 512, 512], P(None, 'rows', 'cols'), may hold values from -4 to 10, as said below
- flags: int32 [16, 32, 32], P('rows', 'cols'), may hold values from 0 to 1, as said below
- owners: int32 [2048, 1], P(('rows', 'cols')), may hold values from 0 to 15; in each aligned block of 16 rows (0 to 15, 16 to 31, ...) at most 2 rows name the same one
Outputs:
- faces_new: float32 [3, 256, 512, 512], P(None, 'rows', 'cols')
- arrivals: float32 [8, 16, 16, 2, 8, 4096], P('rows', 'cols')
The draws below stay inside these ranges and needn't reach their ends.
Inputs may be any that keep to these rules, and one draw needn't show every extreme that they name: `state`: density (field 0) is positive, energy (field 1) lies in 1 to 10. `flags`: each device's 2 x 2 x 32 meshblocks hold exactly 2 flagged ones. `owners`: among the 16 rows of one device, no column is named more than 2 times.
All inputs are finite; a program needn't handle non-finite values.
Results may differ from the reference program's by a relative error of at most 0.0003.
Values sent between devices are 32-bit elements; how exact they have to be, the bound alone decides.
No kernel may reach another device: no remote copies, remote signals or barrier semaphores. Data moves between devices by JAX's collectives and lax.ppermute only.
A program may use at most 320 MiB of HBM per device.

```python
import math
import jax
import jax.numpy as jnp
import numpy as np
from jax import lax

BS = 16
GX = 2
GY = 2
GZ = 32
REF_DEV = 2
CAP = 2
KIDS_DEV = 16
NX = 256
NY = 512
NZ = 512
N_ROWS = 8
N_COLS = 16


def draw_state(key, part):
    subkeys = jax.random.split(key, 4)
    grid_shape = (NX, NY, NZ)
    density = jnp.exp(jax.random.uniform(subkeys[0], grid_shape, jnp.float32, math.log(0.5), math.log(4.0)))
    moment = jnp.clip(jax.random.normal(subkeys[2], (3,) + grid_shape, jnp.float32), -4.0, 4.0)
    face_vals = jnp.clip(jax.random.normal(subkeys[3], (3,) + grid_shape, jnp.float32), -4.0, 4.0)
    energy = jnp.exp(jax.random.uniform(subkeys[1], grid_shape, jnp.float32, 0.0, math.log(10.0)))
    return jnp.concatenate([density[None], energy[None], moment, face_vals], axis=0)


def draw_flags(key, part):
    device_keys = jax.random.split(key, N_ROWS * N_COLS)
    orders = jax.vmap(lambda one_key: jax.random.permutation(one_key, GX * GY * GZ))(device_keys)
    marked = (orders < REF_DEV).astype(jnp.int32)
    marked = marked.reshape(N_ROWS, N_COLS, GX, GY, GZ).transpose(0, 2, 1, 3, 4)
    return marked.reshape(N_ROWS * GX, N_COLS * GY, GZ)


def routed_block(stream_key, own, number, rows, number_of, top, reach, slope):
    ranking = jax.random.permutation(stream_key, number_of)
    crowded, ordinary = portions_of(number_of, rows * top, reach, slope, True), portions_of(number_of, rows * top, reach, slope, False)
    places = jnp.arange(number_of)

    def named(lengths, offset_by):
        used = int((lengths > 0).sum())
        fixed = max(1, used // 4)
        shifted = fixed + (places - fixed + offset_by * (used - fixed)) % max(1, number_of - fixed)
        return jnp.zeros((number_of,), jnp.int32).at[ranking[jnp.where(places < fixed, places, shifted)]].set(jnp.asarray(lengths, jnp.int32))

    lengths = jnp.where(number % 4 == 0, named(crowded, number // 4), named(ordinary, number - number // 4 - 1))
    mixed = jax.random.permutation(jax.random.fold_in(own, 3), number_of)
    donor, receiver = mixed[0:number_of // 2 * 2:2], mixed[1:number_of // 2 * 2:2]
    slack = jnp.minimum(lengths[donor] - 1, reach - lengths[receiver]) // 2
    slack = jnp.where((donor == ranking[0]) | (receiver == ranking[0]) | (lengths[receiver] == 0), 0, jnp.maximum(slack, 0))
    shifted = jax.random.randint(jax.random.fold_in(own, 4), (number_of // 2,), 0, 1 << 20) % (slack + 1)
    lengths = lengths.at[donor].add(-shifted).at[receiver].add(shifted)
    members = jnp.searchsorted(jnp.cumsum(lengths), jnp.arange(rows * top), side="right").astype(jnp.int32)
    grid = members.reshape(top, rows).T
    grid = grid[jax.random.permutation(jax.random.fold_in(own, 1), rows)]
    offset_by = jax.random.randint(jax.random.fold_in(own, 2), (rows, 1), 0, top)
    return jnp.take_along_axis(grid, (jnp.arange(top)[None, :] + offset_by) % top, axis=1)


def portions_of(amount, total, reach, skew, full):
    weights = [(1 << 20) // math.isqrt(standing ** skew) + 1 for standing in range(1, amount + 1)]
    largest = reach if full else min(reach, max(-(-total // amount), total * weights[0] // sum(weights)))
    least = 1 if total - largest >= amount - 1 else 0
    given, rest = [largest] + [least] * (amount - 1), total - largest - least * (amount - 1)
    while rest > 0:
        free = [i for i in range(1, amount) if given[i] < largest] or [i for i in range(1, amount) if given[i] < reach]
        whole, left = sum([weights[i] for i in free]), rest
        for i in free:
            extra = min(reach - given[i], max(1, left * weights[i] // whole), rest)
            given[i] = given[i] + extra
            rest = rest - extra
    return np.array(given)


def setup_inputs(seed: int = 0) -> dict:
    key_of = jax.random.split(jax.random.key(seed), 4)
    state = draw_state(jax.random.fold_in(key_of[3], 71), 0)
    flags = draw_flags(jax.random.fold_in(key_of[3], 71), 0)
    owners_keys = jax.random.split(jax.random.fold_in(key_of[2], 1), (N_ROWS * N_COLS * KIDS_DEV) // KIDS_DEV)
    owners_turns = jax.random.permutation(jax.random.fold_in(key_of[2], 3), (N_ROWS * N_COLS * KIDS_DEV) // KIDS_DEV)
    owners = jax.vmap(lambda own, number: routed_block(jax.random.fold_in(key_of[2], 2), own, number, KIDS_DEV, N_COLS, 1, CAP, 2))(owners_keys, owners_turns).reshape((N_ROWS * N_COLS * KIDS_DEV, 1))
    return dict(state=state, flags=flags, owners=owners)


courant = 0.3


def minmod(left, right):
    return jnp.maximum(jnp.minimum(left, right), 0.0) + jnp.minimum(jnp.maximum(left, right), 0.0)


def advance_faces(padded):
    density = padded[0, 1:-1, 1:-1, 1:-1]
    velocity = padded[2:5, 1:-1, 1:-1, 1:-1] / density
    field_x = 0.5 * (padded[5, 1:-1, 1:-1, 1:-1] + padded[5, 2:, 1:-1, 1:-1])
    field_y = 0.5 * (padded[6, 1:-1, 1:-1, 1:-1] + padded[6, 1:-1, 2:, 1:-1])
    field_z = 0.5 * (padded[7, 1:-1, 1:-1, 1:-1] + padded[7, 1:-1, 1:-1, 2:])
    elec_x = velocity[2] * field_y - velocity[1] * field_z
    elec_y = velocity[0] * field_z - velocity[2] * field_x
    elec_z = velocity[1] * field_x - velocity[0] * field_y
    edge_z = 0.25 * (elec_z[:-1, :-1, 1:-1] + elec_z[:-1, 1:, 1:-1] + elec_z[1:, :-1, 1:-1] + elec_z[1:, 1:, 1:-1])
    edge_y = 0.25 * (elec_y[:-1, 1:-1, :-1] + elec_y[:-1, 1:-1, 1:] + elec_y[1:, 1:-1, :-1] + elec_y[1:, 1:-1, 1:])
    edge_x = 0.25 * (elec_x[1:-1, :-1, :-1] + elec_x[1:-1, :-1, 1:] + elec_x[1:-1, 1:, :-1] + elec_x[1:-1, 1:, 1:])
    face_vals = padded[5:8, 2:-2, 2:-2, 2:-2]
    new_x = face_vals[0] - courant * ((edge_z[:-1, 1:] - edge_z[:-1, :-1]) - (edge_y[:-1, :, 1:] - edge_y[:-1, :, :-1]))
    new_y = face_vals[1] - courant * ((edge_x[:, :-1, 1:] - edge_x[:, :-1, :-1]) - (edge_z[1:, :-1] - edge_z[:-1, :-1]))
    new_z = face_vals[2] - courant * ((edge_y[1:, :, :-1] - edge_y[:-1, :, :-1]) - (edge_x[:, 1:, :-1] - edge_x[:, :-1, :-1]))
    return jnp.stack([new_x, new_y, new_z], axis=0)


def prolong(coarse_piece):
    half_cells = coarse_piece.shape[1] - 2
    centre = coarse_piece[:5, 1:-1, 1:-1, 1:-1]
    slope_x = minmod(coarse_piece[:5, 2:, 1:-1, 1:-1] - centre, centre - coarse_piece[:5, :-2, 1:-1, 1:-1])
    slope_y = minmod(coarse_piece[:5, 1:-1, 2:, 1:-1] - centre, centre - coarse_piece[:5, 1:-1, :-2, 1:-1])
    slope_z = minmod(coarse_piece[:5, 1:-1, 1:-1, 2:] - centre, centre - coarse_piece[:5, 1:-1, 1:-1, :-2])
    offsets = jnp.array([-0.25, 0.25], jnp.float32)
    fine_cells = (centre[:, :, None, :, None, :, None]
                  + offsets.reshape(1, 1, 2, 1, 1, 1, 1) * slope_x[:, :, None, :, None, :, None]
                  + offsets.reshape(1, 1, 1, 1, 2, 1, 1) * slope_y[:, :, None, :, None, :, None]
                  + offsets.reshape(1, 1, 1, 1, 1, 1, 2) * slope_z[:, :, None, :, None, :, None])
    fine_cells = fine_cells.reshape(5, -1)
    fine_shape = (half_cells, 2, half_cells, 2, half_cells, 2)
    face_x = coarse_piece[5, 1:, 1:-1, 1:-1]
    fine_x = jnp.stack([face_x[:-1], 0.5 * (face_x[:-1] + face_x[1:])], axis=1)[:, :, :, None, :, None]
    face_y = coarse_piece[6, 1:-1, 1:, 1:-1]
    fine_y = jnp.stack([face_y[:, :-1], 0.5 * (face_y[:, :-1] + face_y[:, 1:])], axis=2)[:, None, :, :, :, None]
    face_z = coarse_piece[7, 1:-1, 1:-1, 1:]
    fine_z = jnp.stack([face_z[:, :, :-1], 0.5 * (face_z[:, :, :-1] + face_z[:, :, 1:])], axis=3)[:, None, :, None, :, :]
    fine_faces = jnp.stack([jnp.broadcast_to(fine_x, fine_shape), jnp.broadcast_to(fine_y, fine_shape),
                            jnp.broadcast_to(fine_z, fine_shape)], axis=0).reshape(3, -1)
    return jnp.concatenate([fine_cells, fine_faces], axis=0)


def child_slots(flag_list, owner_list, column_count):
    block_count = flag_list.shape[0]
    parent_count = owner_list.shape[0] // 8
    running = jnp.cumsum(flag_list).astype(jnp.int32)
    rank_ids = jnp.arange(parent_count, dtype=jnp.int32)
    matches = (flag_list[None, :] == 1) & (running[None, :] == rank_ids[:, None] + 1)
    position = jnp.sum(jnp.where(matches, jnp.arange(block_count, dtype=jnp.int32)[None, :], 0), axis=1).astype(jnp.int32)
    onehot = (owner_list[:, None] == jnp.arange(column_count, dtype=jnp.int32)[None, :]).astype(jnp.int32)
    earlier = jnp.cumsum(onehot, axis=0).astype(jnp.int32) - onehot
    order_rank = jnp.sum(earlier * onehot, axis=1).astype(jnp.int32)
    return position, (owner_list * CAP + order_rank).astype(jnp.int32)


def piece_starts(position, blocks_y, blocks_z, base_x, base_y):
    child_ids = jnp.arange(position.shape[0] * 8, dtype=jnp.int32)
    parent_pos = position[child_ids // 8]
    octant = child_ids % 8
    half_cells = BS // 2
    start_x = base_x + BS * (parent_pos // (blocks_y * blocks_z)) + half_cells * (octant // 4) + 1
    start_y = base_y + BS * ((parent_pos // blocks_z) % blocks_y) + half_cells * ((octant // 2) % 2) + 1
    start_z = BS * (parent_pos % blocks_z) + half_cells * (octant % 2) + 1
    return start_x.astype(jnp.int32), start_y.astype(jnp.int32), start_z.astype(jnp.int32)


def cut_pieces(padded, start_x, start_y, start_z):
    piece_span = BS // 2 + 2

    def one_piece(corner_x, corner_y, corner_z):
        anchor = jnp.zeros((), jnp.int32)
        return lax.dynamic_slice(padded, (anchor, corner_x, corner_y, corner_z), (8, piece_span, piece_span, piece_span))

    return jax.vmap(one_piece)(start_x, start_y, start_z)


def reference(state, flags, owners):
    margins = ((0, 0), (2, 2), (2, 2), (2, 2))
    padded = jnp.concatenate([jnp.pad(state[:1], margins, constant_values=1.0), jnp.pad(state[1:], margins)], axis=0)
    width_x = GX * BS
    width_y = GY * BS

    def slab(row_id):
        slab_view = lax.dynamic_slice_in_dim(padded, row_id * width_x, width_x + 4, 1)
        return advance_faces(slab_view)

    slabs = lax.map(slab, jnp.arange(N_ROWS, dtype=jnp.int32))
    faces_new = jnp.transpose(slabs, (1, 0, 2, 3, 4)).reshape(3, N_ROWS * width_x, N_COLS * width_y, GZ * BS)

    def device_buffer(device_id):
        row_id = device_id // N_COLS
        col_id = device_id % N_COLS
        flag_view = lax.dynamic_slice(flags, (row_id * GX, col_id * GY, jnp.zeros((), jnp.int32)), (GX, GY, GZ)).reshape(-1)
        owner_view = lax.dynamic_slice_in_dim(owners[:, 0], device_id * KIDS_DEV, KIDS_DEV)
        position, slot_index = child_slots(flag_view, owner_view, N_COLS)
        start_x, start_y, start_z = piece_starts(position, GY, GZ, row_id * width_x, col_id * width_y)
        pieces = cut_pieces(padded, start_x, start_y, start_z)
        children = jax.vmap(prolong)(pieces)
        return jnp.zeros((N_COLS * CAP,) + children.shape[1:], jnp.float32).at[slot_index].set(children)

    buffers = lax.map(device_buffer, jnp.arange(N_ROWS * N_COLS, dtype=jnp.int32))
    arrivals = buffers.reshape(N_ROWS, N_COLS, N_COLS, CAP, 8, BS ** 3).transpose(0, 2, 1, 3, 4, 5)
    return faces_new, arrivals
```

```python
import functools

import jax
import jax.numpy as jnp
import numpy as np
from jax import lax
from jax.experimental import pallas as pl
from jax.experimental.pallas import tpu as pltpu
from jax.sharding import PartitionSpec as P

F32 = jnp.float32
BF16 = jnp.bfloat16
BS = 16
CAP = 2
PARENTS = 2
KIDS = 16
LANES = 128
LIMIT = 60 * 1024 * 1024

courant = 0.3
SCALE = 0.25 * 0.5 * courant


def even_swap(count):
    return [(i, i ^ 1) for i in range(count)]


def odd_swap(count):
    return [p for i in range(1, count - 1, 2) for p in ((i, i + 1), (i + 1, i))]


def flat_rows(ref):
    rows = 1
    for n in ref.shape[:-1]:
        rows *= n
    return ref.reshape(rows, ref.shape[-1])


def pack_cols_kernel(place, state, even_ref, odd_ref, tiles, sems):
    nx, ny = state.shape[1], state.shape[2]
    nk = state.shape[3] // LANES
    copies = []
    for side in range(2):
        for k in range(nk):
            copies.append(
                pltpu.make_async_copy(
                    state.at[:, :, pl.ds(side * (ny - 8), 8), pl.ds(k * LANES, LANES)],
                    tiles.at[side, k],
                    sems.at[side, k],
                )
            )
    for c in copies:
        c.start()
    for c in copies:
        c.wait()
    high_in_even = place[1] == 0
    for k in range(nk):
        cut = slice(k * LANES, (k + 1) * LANES)
        low_tile = flat_rows(tiles.at[0, k])
        high_tile = flat_rows(tiles.at[1, k])
        for layer in range(9):
            field = layer if layer < 8 else 6
            at_low = field * nx * 8 + (0 if layer < 8 else 1)
            at_high = field * nx * 8 + (7 if layer < 8 else 6)
            low = low_tile[pl.ds(at_low, nx, stride=8), :]
            high = high_tile[pl.ds(at_high, nx, stride=8), :]
            even_ref[layer, :, cut] = jnp.where(high_in_even, high, low)
            odd_ref[layer, :, cut] = jnp.where(high_in_even, low, high)


def pack_cols(place, state):
    fields, nx, ny, nz = state.shape
    shape = jax.ShapeDtypeStruct((fields + 1, nx, nz), F32)
    return pl.pallas_call(
        pack_cols_kernel,
        out_shape=[shape, shape],
        in_specs=[pl.BlockSpec(memory_space=pltpu.SMEM), pl.BlockSpec(memory_space=pl.ANY)],
        out_specs=[pl.BlockSpec(memory_space=pltpu.VMEM)] * 2,
        scratch_shapes=[
            pltpu.VMEM((2, nz // LANES, fields, nx, 8, LANES), F32),
            pltpu.SemaphoreType.DMA((2, nz // LANES)),
        ],
        compiler_params=pltpu.CompilerParams(vmem_limit_bytes=LIMIT),
        name="pack_cols",
    )(place, state)


def pack_rows_kernel(place, state, even_ref, odd_ref, sems):
    nx = state.shape[1]
    at_even = jnp.where(place[0] == 0, nx - 1, 0)
    at_odd = nx - 1 - at_even
    copies = []
    for number, (ref, at) in enumerate(((even_ref, at_even), (odd_ref, at_odd))):
        second = jnp.where(at == 0, 1, nx - 2)
        copies.append(
            pltpu.make_async_copy(state.at[:, at], ref.at[pl.ds(0, 8)], sems.at[number, 0])
        )
        copies.append(pltpu.make_async_copy(state.at[5, second], ref.at[8], sems.at[number, 1]))
    for c in copies:
        c.start()
    for c in copies:
        c.wait()


def pack_rows(place, state):
    fields, nx, ny, nz = state.shape
    shape = jax.ShapeDtypeStruct((fields + 1, ny, nz), F32)
    return pl.pallas_call(
        pack_rows_kernel,
        out_shape=[shape, shape],
        in_specs=[pl.BlockSpec(memory_space=pltpu.SMEM), pl.BlockSpec(memory_space=pl.ANY)],
        out_specs=[pl.BlockSpec(memory_space=pltpu.VMEM)] * 2,
        scratch_shapes=[pltpu.SemaphoreType.DMA((2, 2))],
        compiler_params=pltpu.CompilerParams(vmem_limit_bytes=LIMIT),
        name="pack_rows",
    )(place, state)


def lane_up(parts, lane):
    rolled = [pltpu.roll(p, LANES - 1, 1) for p in parts]
    rolled.append(jnp.zeros_like(parts[0]))
    return [jnp.where(lane == LANES - 1, rolled[k + 1], rolled[k]) for k in range(len(parts))]


def lane_down(parts, lane):
    rolled = [pltpu.roll(p, 1, 1) for p in parts]
    rolled = [jnp.zeros_like(parts[0])] + rolled
    return [jnp.where(lane == 0, rolled[k], rolled[k + 1]) for k in range(len(parts))]


def advance_kernel(
    place, state, row_even, row_odd, col_even, col_odd, cor_even, cor_odd,
    out, dens, flds, rims, rim_e, edge, prev, done, in_sems, halo_sems, out_sems,
):
    nx, ny, nz = state.shape[1:]
    nk = nz // LANES
    chunk = 4
    chunks = nx // chunk
    row_par, col_par = place[0], place[1]

    def cut(k):
        return slice(k * LANES, (k + 1) * LANES)

    def chunk_in(c):
        at = pl.ds(c * chunk, chunk)
        to = pl.ds(1 + c * chunk, chunk)
        return (
            pltpu.make_async_copy(state.at[0, at], dens.at[to], in_sems.at[c, 0]),
            pltpu.make_async_copy(state.at[pl.ds(2, 6), at], flds.at[:, to], in_sems.at[c, 1]),
        )

    def rows_in(source, side):
        to = 0 if side == 0 else nx + 1
        copies = [
            pltpu.make_async_copy(source.at[0], dens.at[to], halo_sems.at[side, 0]),
            pltpu.make_async_copy(source.at[pl.ds(2, 6)], flds.at[:, to], halo_sems.at[side, 1]),
        ]
        if side == 1:
            copies.append(
                pltpu.make_async_copy(source.at[8], flds.at[3, nx + 2], halo_sems.at[side, 2])
            )
        return copies

    def cols_in(source, side):
        return [pltpu.make_async_copy(source, rims.at[side, :, pl.ds(8, nx)], halo_sems.at[side, 3])]

    def corner_in(source, half, side, end):
        to = pl.ds(0 if end == 0 else nx + 8, 8)
        return [
            pltpu.make_async_copy(source.at[half], rims.at[side, :, to], halo_sems.at[side, 4 + end])
        ]

    for side in range(2):
        @pl.when(row_par == side)
        def _():
            for c in rows_in(row_odd, side):
                c.start()

        @pl.when(row_par != side)
        def _():
            for c in rows_in(row_even, side):
                c.start()

        @pl.when(col_par == side)
        def _():
            for c in cols_in(col_odd, side):
                c.start()

        @pl.when(col_par != side)
        def _():
            for c in cols_in(col_even, side):
                c.start()

        half = jnp.where(col_par == side, 1, 0)
        for end in range(2):
            @pl.when(row_par == end)
            def _():
                for c in corner_in(cor_odd, half, side, end):
                    c.start()

            @pl.when(row_par != end)
            def _():
                for c in corner_in(cor_even, half, side, end):
                    c.start()

    for c in range(chunks):
        for copy in chunk_in(c):
            copy.start()

    for side in range(2):
        for c in rows_in(row_even, side) + cols_in(col_even, side):
            c.wait()
        for end in range(2):
            for c in corner_in(cor_even, 0, side, end):
                c.wait()

    lane = lax.broadcasted_iota(jnp.int32, (ny, LANES), 1)
    row = lax.broadcasted_iota(jnp.int32, (ny, LANES), 0)

    for at in (0, nx + 1):
        dens[at] = jnp.where(dens[at] > 0.0, dens[at], 1.0)

    span = rims.shape[2]
    rim_lane = lax.broadcasted_iota(jnp.int32, (span, LANES), 1)
    for side in range(2):
        face_z = [rims[side, 7, :, cut(k)] for k in range(nk)]
        face_z_up = lane_up(face_z, rim_lane)
        for k in range(nk):
            rho = rims[side, 0, :, cut(k)]
            inv = SCALE / jnp.where(rho > 0.0, rho, 1.0)
            vel_x = rims[side, 2, :, cut(k)] * inv
            vel_y = rims[side, 3, :, cut(k)] * inv
            vel_z = rims[side, 4, :, cut(k)] * inv
            face_x = rims[side, 5, :, cut(k)]
            mag_x = face_x + pltpu.roll(face_x, span - 1, 0)
            mag_z = face_z[k] + face_z_up[k]
            mag_y = rims[side, 6, :, cut(k)]
            if side == 1:
                rim_e[3, 0, k] = mag_y
                mag_y = mag_y + rims[side, 8, :, cut(k)]
            rim_e[side, 0, k] = vel_y * mag_x - vel_x * mag_y
            rim_e[side, 1, k] = vel_z * mag_y - vel_y * mag_z
            if side == 0:
                rim_e[2, 0, k] = vel_x
                rim_e[2, 1, k] = vel_z

    prev[...] = jnp.zeros_like(prev)

    def plane(p, carry):
        @pl.when((p % chunk == 0) & (p < nx))
        def _():
            for copy in chunk_in(p // chunk):
                copy.wait()

        at_rim = pl.ds(p + 7, 1)
        face_z = [flds[5, p, :, cut(k)] for k in range(nk)]
        face_z_up = lane_up(face_z, lane)
        elec_y = []
        for k in range(nk):
            inv = SCALE / dens[p, :, cut(k)]
            vel_x = flds[0, p, :, cut(k)] * inv
            vel_y = flds[1, p, :, cut(k)] * inv
            vel_z = flds[2, p, :, cut(k)] * inv
            face_y = flds[4, p, :, cut(k)]
            mag_x = flds[3, p, :, cut(k)] + flds[3, p + 1, :, cut(k)]
            above = jnp.where(
                row == ny - 1, rim_e[3, 0, k, at_rim], pltpu.roll(face_y, ny - 1, 0)
            )
            mag_y = face_y + above
            mag_z = face_z[k] + face_z_up[k]
            edge[0, k, 8 : ny + 8] = vel_y * mag_x - vel_x * mag_y
            edge[1, k, 8 : ny + 8] = vel_z * mag_y - vel_y * mag_z
            elec_y.append(vel_x * mag_z - vel_z * mag_x)
            first = face_y[0:1]
            edge[0, k, 7:8] = rim_e[0, 0, k, at_rim] - rim_e[2, 0, k, at_rim] * first
            edge[1, k, 7:8] = rim_e[0, 1, k, at_rim] + rim_e[2, 1, k, at_rim] * first
            edge[0, k, ny + 8 : ny + 9] = rim_e[1, 0, k, at_rim]
            edge[1, k, ny + 8 : ny + 9] = rim_e[1, 1, k, at_rim]
        y_down = lane_down(elec_y, lane)
        y_up = lane_up(elec_y, lane)
        before = jnp.maximum(p - 1, 0)
        for k in range(nk):
            z_below = edge[0, k, 7 : ny + 7]
            z_here = edge[0, k, 8 : ny + 8]
            z_above = edge[0, k, 9 : ny + 9]
            turn = (z_above - z_below) - (y_up[k] - y_down[k])
            z_sum = z_below + z_here
            y_sum = y_down[k] + elec_y[k]
            done[0, p, :, cut(k)] = flds[3, p, :, cut(k)] - (prev[0, k] + turn)
            done[1, before, :, cut(k)] = done[1, before, :, cut(k)] + z_sum
            done[2, before, :, cut(k)] = done[2, before, :, cut(k)] - y_sum
            done[1, p, :, cut(k)] = flds[4, p, :, cut(k)] - prev[1, k]
            done[2, p, :, cut(k)] = face_z[k] + prev[2, k]
            prev[0, k] = turn
            prev[1, k] = z_sum
            prev[2, k] = y_sum
        x_sum = []
        x_diff = []
        for k in range(nk):
            below = edge[1, k, 7 : ny + 7]
            x_sum.append(below + edge[1, k, 8 : ny + 8])
            x_diff.append(edge[1, k, 9 : ny + 9] - below)
        sum_down = lane_down(x_sum, lane)
        sum_up = lane_up(x_sum, lane)
        diff_down = lane_down(x_diff, lane)
        for k in range(nk):
            done[1, p, :, cut(k)] = done[1, p, :, cut(k)] - (sum_up[k] - sum_down[k])
            done[2, p, :, cut(k)] = done[2, p, :, cut(k)] + (diff_down[k] + x_diff[k])

        @pl.when((p > chunk) & ((p - 1) % chunk == 0))
        def _():
            chunk_out((p - 1) // chunk - 1).start()

        return carry

    def chunk_out(c):
        return pltpu.make_async_copy(
            done.at[:, pl.ds(1 + c * chunk, chunk)],
            out.at[:, pl.ds(c * chunk, chunk)],
            out_sems.at[c],
        )

    lax.fori_loop(0, nx + 2, plane, 0)
    for c in range(chunks):
        chunk_out(c).wait()


def advance(place, state, rows_halo, cols_halo, corners):
    nx, ny, nz = state.shape[1:]
    nk = nz // LANES
    any_space = pl.BlockSpec(memory_space=pl.ANY)
    return pl.pallas_call(
        advance_kernel,
        out_shape=jax.ShapeDtypeStruct((3, nx, ny, nz), F32),
        in_specs=[pl.BlockSpec(memory_space=pltpu.SMEM)] + [any_space] * 7,
        out_specs=any_space,
        scratch_shapes=[
            pltpu.VMEM((nx + 2, ny, nz), F32),
            pltpu.VMEM((6, nx + 3, ny, nz), F32),
            pltpu.VMEM((2, 9, nx + 16, nz), F32),
            pltpu.VMEM((4, 2, nk, nx + 16, LANES), F32),
            pltpu.VMEM((2, nk, ny + 16, LANES), F32),
            pltpu.VMEM((3, nk, ny, LANES), F32),
            pltpu.VMEM((3, nx + 2, ny, nz), F32),
            pltpu.SemaphoreType.DMA((nx // 4, 2)),
            pltpu.SemaphoreType.DMA((2, 6)),
            pltpu.SemaphoreType.DMA((nx // 4,)),
        ],
        compiler_params=pltpu.CompilerParams(vmem_limit_bytes=LIMIT),
        cost_estimate=pl.CostEstimate(
            flops=60 * nx * ny * nz, bytes_accessed=40 * nx * ny * nz, transcendentals=0
        ),
        name="advance",
    )(place, state, *rows_halo, *cols_halo, *corners)


SIDE = BS // 2 + 2
WIDE = BS + 2


def pieces_kernel(
    place, parent, slots, state, row_even, row_odd, col_even, col_odd, out, window, rim, sems
):
    nx, ny, nz = state.shape[1:]
    nk = nz // LANES
    row_par, col_par = place[0], place[1]
    spots = []
    for r in range(PARENTS):
        ix, iy, kz = parent[3 * r], parent[3 * r + 1], parent[3 * r + 2]
        begin = kz * BS - 1
        tile = (begin + LANES) // LANES - 1
        shift = begin - tile * LANES
        y_from = pl.multiple_of(8 * iy, 8)
        y_to = pl.multiple_of(8 - 8 * iy, 8)
        waits = []
        for t in range(2):
            column = jnp.clip(tile + t, 0, nk - 1)
            z_at = pl.ds(pl.multiple_of(column * LANES, LANES), LANES)
            body = pltpu.make_async_copy(
                state.at[:, pl.ds((BS - 1) * ix, BS + 1), pl.ds(y_from, 24), z_at],
                window.at[r, t, :, pl.ds(1 - ix, BS + 1), pl.ds(y_to, 24)],
                sems.at[r, t, 0],
            )
            body.start()

            def row_copy(source):
                return pltpu.make_async_copy(
                    source.at[pl.ds(0, 8), pl.ds(y_from, 24), z_at],
                    window.at[r, t, :, (WIDE - 1) * ix, pl.ds(y_to, 24)],
                    sems.at[r, t, 1],
                )

            def col_copy(source):
                return pltpu.make_async_copy(
                    source.at[pl.ds(0, 8), pl.ds(pl.multiple_of(ix * BS, BS), BS), z_at],
                    rim.at[r, t],
                    sems.at[r, t, 2],
                )

            @pl.when(ix != row_par)
            def _():
                row_copy(row_even).start()

            @pl.when(ix == row_par)
            def _():
                row_copy(row_odd).start()

            @pl.when(iy != col_par)
            def _():
                col_copy(col_even).start()

            @pl.when(iy == col_par)
            def _():
                col_copy(col_odd).start()

            waits += [body, row_copy(row_even), col_copy(col_even)]
        spots.append((iy, kz, shift, waits))

    out[...] = jnp.zeros_like(out)
    lane = lax.broadcasted_iota(jnp.int32, (8, LANES), 1)
    sub = lax.broadcasted_iota(jnp.int32, (8, LANES), 0)
    filler = jnp.where(sub == 0, 1.0, 0.0)
    for r in range(PARENTS):
        iy, kz, shift, waits = spots[r]
        for w in waits:
            w.wait()
        for t in range(2):
            for at in (0, WIDE - 1):
                rho = window[r, t, 0, at]
                window[r, t, 0, at] = jnp.where(rho > 0.0, rho, 1.0)
        turn = LANES - shift
        first = lane < turn
        outside = ((kz == 0) & (lane == 0)) | ((kz == nz // BS - 1) & (lane == WIDE - 1))
        flat = [flat_rows(window.at[r, t]) for t in range(2)]
        flat_rim = [flat_rows(rim.at[r, t]) for t in range(2)]

        def plane(i, carry):
            inside = (i > 0) & (i < WIDE - 1)
            rim_row = jnp.clip(i - 1, 0, BS - 1)
            sums = [jnp.zeros((8, LANES), F32) for _ in range(4)]
            for j in range(WIDE):
                halves = []
                for t in range(2):
                    value = flat[t][pl.ds(i * 32 + j + 7, 8, stride=WIDE * 32), :]
                    if j == 0 or j == WIDE - 1:
                        beside = flat_rim[t][pl.ds(rim_row, 8, stride=BS), :]
                        beside = jnp.where((sub == 0) & (beside == 0.0), 1.0, beside)
                        from_rim = iy == (0 if j == 0 else 1)
                        value = jnp.where(from_rim, beside, value)
                        value = jnp.where(inside, value, 0.0)
                    halves.append(pltpu.roll(value, turn, 1))
                value = jnp.where(first, halves[0], halves[1])
                value = jnp.where(outside, filler, value)
                parts = (
                    jnp.where(lane < SIDE, value, 0.0),
                    jnp.where((lane >= BS // 2) & (lane < WIDE), value, 0.0),
                )
                for b in range(2):
                    row = j - 8 * b
                    if 0 <= row < SIDE:
                        for c in range(2):
                            amount = (row * SIDE - 8 * c) % LANES
                            moved = pltpu.roll(parts[c], amount, 1) if amount else parts[c]
                            sums[2 * b + c] = sums[2 * b + c] + moved
            for b in range(2):
                for c in range(2):
                    for a in range(2):
                        number = 8 * r + 4 * a + 2 * b + c

                        @pl.when((i >= 8 * a) & (i < 8 * a + SIDE))
                        def _():
                            at = pl.multiple_of((i - 8 * a) * 8, 8)
                            out[slots[number], pl.ds(at, 8)] = sums[2 * b + c]

            return carry

        lax.fori_loop(0, WIDE, plane, 0)


def pieces(place, parent, slots, state, rows_halo, cols_halo, count):
    smem = pl.BlockSpec(memory_space=pltpu.SMEM)
    any_space = pl.BlockSpec(memory_space=pl.ANY)
    return pl.pallas_call(
        pieces_kernel,
        out_shape=jax.ShapeDtypeStruct((count * CAP, SIDE * 8, LANES), F32),
        in_specs=[smem] * 3 + [any_space] * 5,
        out_specs=pl.BlockSpec(memory_space=pltpu.VMEM),
        scratch_shapes=[
            pltpu.VMEM((PARENTS, 2, 8, WIDE, 32, LANES), F32),
            pltpu.VMEM((PARENTS, 2, 8, BS, LANES), F32),
            pltpu.SemaphoreType.DMA((PARENTS, 2, 3)),
        ],
        compiler_params=pltpu.CompilerParams(vmem_limit_bytes=LIMIT),
        name="pieces",
    )(place, parent, slots, state, *rows_halo, *cols_halo)


def spread_weights():
    spread = np.zeros((3, LANES, 256), np.float32)
    for y in range(BS):
        for z in range(BS):
            at = (y // 2 + 1) * SIDE + z // 2 + 1
            spread[0, at, y * BS + z] = 1.0
            spread[1, at, y * BS + z] = 0.25 * (2 * (y % 2) - 1)
            spread[2, at, y * BS + z] = 0.25 * (2 * (z % 2) - 1)
    return spread


def limited(left, right):
    return jnp.maximum(jnp.minimum(left, right), 0.0) + jnp.minimum(jnp.maximum(left, right), 0.0)


def thirds(value):
    top = value.astype(BF16)
    rest = value - top.astype(F32)
    middle = rest.astype(BF16)
    return top, middle, (rest - middle.astype(F32)).astype(BF16)


def prolong_kernel(weights, piece, out, low, high, side):
    count = piece.shape[0]
    sub = lax.broadcasted_iota(jnp.int32, (64, LANES), 0) % 8
    cells = sub < 5

    def slopes(s, carry):
        here = piece[s, 8:72]
        x_up = piece[s, 16:80] - here
        x_down = here - piece[s, 0:64]
        y_up = pltpu.roll(here, LANES - SIDE, 1) - here
        y_down = here - pltpu.roll(here, SIDE, 1)
        z_up = pltpu.roll(here, LANES - 1, 1) - here
        z_down = here - pltpu.roll(here, 1, 1)
        slope_x = jnp.where(cells, limited(x_up, x_down), jnp.where(sub == 5, x_up, 0.0))
        slope_y = jnp.where(cells, limited(y_up, y_down), jnp.where(sub == 6, y_up, 0.0))
        slope_z = jnp.where(cells, limited(z_up, z_down), jnp.where(sub == 7, z_up, 0.0))
        middle = here + jnp.where(cells, 0.0, 0.25 * (slope_x + slope_y + slope_z))
        at = pl.ds(pl.multiple_of(s * 64, 64), 64)
        low[at] = middle - 0.25 * slope_x
        high[at] = middle + 0.25 * slope_x
        side[at, 0:LANES] = slope_y
        side[at, LANES:] = slope_z
        return carry

    lax.fori_loop(0, count, slopes, 0)
    spread = weights[0]
    both = weights[1:3].reshape(2 * LANES, 256)

    def times(value, matrix):
        return sum(jnp.dot(v, matrix, preferred_element_type=F32) for v in thirds(value))

    for s in range(count):
        at = slice(s * 64, (s + 1) * 64)
        tilt = times(side[at], both)
        for p, half in enumerate((low, high)):
            fine = times(half[at], spread) + tilt
            for i in range(8):
                x = 2 * i + p
                out[0, 0, s // 2, s % 2, :, x * 256 : (x + 1) * 256] = fine[8 * i : 8 * i + 8]


def prolong(received, count):
    group = 8
    return pl.pallas_call(
        prolong_kernel,
        grid=(count * CAP // group,),
        out_shape=jax.ShapeDtypeStruct((1, 1, count, CAP, 8, BS**3), F32),
        in_specs=[
            pl.BlockSpec((3, LANES, 256), lambda g: (0, 0, 0)),
            pl.BlockSpec((group, SIDE * 8, LANES), lambda g: (g, 0, 0)),
        ],
        out_specs=pl.BlockSpec(
            (1, 1, group // CAP, CAP, 8, BS**3), lambda g: (0, 0, g, 0, 0, 0)
        ),
        scratch_shapes=[
            pltpu.VMEM((group * 64, LANES), F32),
            pltpu.VMEM((group * 64, LANES), F32),
            pltpu.VMEM((group * 64, 2 * LANES), F32),
        ],
        compiler_params=pltpu.CompilerParams(vmem_limit_bytes=LIMIT),
        name="prolong",
    )(jnp.asarray(spread_weights(), BF16), received)


def find_parents(flags):
    gx, gy, gz = flags.shape
    where = jnp.arange(gx * gy * gz, dtype=jnp.int32).reshape(flags.shape)
    first = jnp.min(jnp.where(flags == 1, where, gx * gy * gz - 1))
    last = jnp.max(jnp.where(flags == 1, where, 0))
    at = jnp.stack([first, last])
    return jnp.stack([at // (gy * gz), at // gz % gy, at % gz], axis=1).reshape(-1)


def find_slots(owners):
    same = owners[:, None] == owners[None, :]
    number = jnp.arange(owners.shape[0])
    earlier = same & (number[None, :] < number[:, None])
    return owners * CAP + jnp.sum(earlier.astype(jnp.int32), axis=1)


def on_device(state, flags, owners):
    rows, cols = lax.axis_size("rows"), lax.axis_size("cols")
    place = jnp.stack([lax.axis_index("rows") % 2, lax.axis_index("cols") % 2]).astype(jnp.int32)
    col_even, col_odd = pack_cols(place, state)
    col_even = lax.ppermute(col_even, "cols", even_swap(cols))
    col_odd = lax.ppermute(col_odd, "cols", odd_swap(cols))
    row_even, row_odd = pack_rows(place, state)
    row_even = lax.ppermute(row_even, "rows", even_swap(rows))
    row_odd = lax.ppermute(row_odd, "rows", odd_swap(rows))

    parent = find_parents(flags)
    slots = find_slots(owners[:, 0])
    sent = pieces(
        place, parent, slots, state, (row_even, row_odd), (col_even, col_odd), cols
    )
    received = lax.all_to_all(
        sent.reshape((cols, CAP) + sent.shape[1:]), "cols", split_axis=0, concat_axis=0, tiled=True
    )

    both = jnp.stack([col_even, col_odd])
    low, high = both[:, :, :8], both[:, :, -8:]
    cor_even = lax.ppermute(jnp.where(place[0] == 0, high, low), "rows", even_swap(rows))
    cor_odd = lax.ppermute(jnp.where(place[0] == 0, low, high), "rows", odd_swap(rows))
    faces_new = advance(
        place, state, (row_even, row_odd), (col_even, col_odd), (cor_even, cor_odd)
    )
    arrivals = prolong(received.reshape(sent.shape), cols)
    return faces_new, arrivals


def solution(mesh):
    return jax.shard_map(
        on_device,
        mesh=mesh,
        in_specs=(
            P(None, "rows", "cols", None),
            P("rows", "cols", None),
            P(("rows", "cols"), None),
        ),
        out_specs=(P(None, "rows", "cols", None), P("rows", "cols", None, None, None, None)),
        check_vma=False,
    )
```

```python
import functools

import jax
import jax.numpy as jnp
import numpy as np
from jax import lax
from jax.experimental import pallas as pl
from jax.experimental.pallas import tpu as pltpu
from jax.sharding import PartitionSpec as P

F32 = jnp.float32
BF16 = jnp.bfloat16
BS = 16
CAP = 2
PARENTS = 2
KIDS = 16
LANES = 128
MIB = 1024 * 1024
ANY = pl.BlockSpec(memory_space=pl.ANY)
SMEM = pl.BlockSpec(memory_space=pltpu.SMEM)

courant = 0.3
SCALE = 0.25 * 0.5 * courant


def even_swap(count):
    return [(i, i ^ 1) for i in range(count)]


def odd_swap(count):
    return [p for i in range(1, count - 1, 2) for p in ((i, i + 1), (i + 1, i))]


def flat_rows(ref):
    rows = 1
    for n in ref.shape[:-1]:
        rows *= n
    return ref.reshape(rows, ref.shape[-1])


def parity(axis):
    return lax.rem(lax.axis_index(axis), 2)


def pack_kernel(state, row_even, row_odd, col_even, col_odd, tiles, rims, row_sems, sems, out_sems):
    nx, ny = state.shape[1], state.shape[2]
    nk = state.shape[3] // LANES

    def tile_in(side, k, f):
        return pltpu.make_async_copy(
            state.at[pl.ds(f, 2), :, pl.ds(side * (ny - 8), 8), pl.ds(k * LANES, LANES)],
            tiles.at[side, k, pl.ds(f, 2)],
            sems.at[side, k, f],
        )

    for k in range(nk):
        for side in range(2):
            for f in range(0, 8, 2):
                tile_in(side, k, f).start()
    at_even = jnp.where(parity("rows") == 0, nx - 1, 0)
    at_odd = nx - 1 - at_even
    row_copies = []
    for number, (ref, at) in enumerate(((row_even, at_even), (row_odd, at_odd))):
        second = jnp.where(at == 0, 1, nx - 2)
        row_copies.append(
            pltpu.make_async_copy(state.at[:, at], ref.at[pl.ds(0, 8)], row_sems.at[number, 0])
        )
        row_copies.append(
            pltpu.make_async_copy(state.at[5, second], ref.at[8], row_sems.at[number, 1])
        )
    for c in row_copies:
        c.start()
    high_in_even = parity("cols") == 0
    outs = []
    for k in range(nk):
        for side in range(2):
            for f in range(0, 8, 2):
                tile_in(side, k, f).wait()
        low_tile = flat_rows(tiles.at[0, k])
        high_tile = flat_rows(tiles.at[1, k])
        for layer in range(9):
            field = layer if layer < 8 else 6
            at_low = field * nx * 8 + (0 if layer < 8 else 1)
            at_high = field * nx * 8 + (7 if layer < 8 else 6)
            low = low_tile[pl.ds(at_low, nx, stride=8), :]
            high = high_tile[pl.ds(at_high, nx, stride=8), :]
            rims[0, k, layer] = jnp.where(high_in_even, high, low)
            rims[1, k, layer] = jnp.where(high_in_even, low, high)
        for number, ref in enumerate((col_even, col_odd)):
            c = pltpu.make_async_copy(
                rims.at[number, k],
                ref.at[:, :, pl.ds(k * LANES, LANES)],
                out_sems.at[number, k],
            )
            c.start()
            outs.append(c)
    for c in row_copies + outs:
        c.wait()


def pack(state):
    fields, nx, ny, nz = state.shape
    nk = nz // LANES
    row_shape = jax.ShapeDtypeStruct((fields + 1, ny, nz), F32)
    col_shape = jax.ShapeDtypeStruct((fields + 1, nx, nz), F32)
    return pl.pallas_call(
        pack_kernel,
        out_shape=[row_shape, row_shape, col_shape, col_shape],
        in_specs=[ANY],
        out_specs=[pl.BlockSpec(memory_space=pltpu.VMEM)] * 2 + [ANY] * 2,
        scratch_shapes=[
            pltpu.VMEM((2, nk, fields, nx, 8, LANES), F32),
            pltpu.VMEM((2, nk, fields + 1, nx, LANES), F32),
            pltpu.SemaphoreType.DMA((2, 2)),
            pltpu.SemaphoreType.DMA((2, nk, fields)),
            pltpu.SemaphoreType.DMA((2, nk)),
        ],
        compiler_params=pltpu.CompilerParams(vmem_limit_bytes=50 * MIB),
        name="pack",
    )(state)


def lane_up(parts, lane):
    rolled = [pltpu.roll(p, LANES - 1, 1) for p in parts]
    rolled.append(jnp.zeros_like(parts[0]))
    return [jnp.where(lane == LANES - 1, rolled[k + 1], rolled[k]) for k in range(len(parts))]


def lane_down(parts, lane):
    rolled = [pltpu.roll(p, 1, 1) for p in parts]
    rolled = [jnp.zeros_like(parts[0])] + rolled
    return [jnp.where(lane == 0, rolled[k], rolled[k + 1]) for k in range(len(parts))]


def scaled_inverse(rho):
    guess = pl.reciprocal(rho, approx=True)
    guess = guess * (2.0 - rho * guess)
    guess = guess * (2.0 - rho * guess)
    return SCALE * guess


def advance_kernel(
    state, row_even, row_odd, col_even, col_odd, cor_even, cor_odd,
    out, dens, flds, rims, rim_e, edge, prev, done, in_sems, halo_sems, out_sems,
):
    nx, ny, nz = state.shape[1:]
    nk = nz // LANES
    chunk = 4
    chunks = nx // chunk
    ahead = 3
    row_par, col_par = parity("rows"), parity("cols")

    def cut(k):
        return slice(k * LANES, (k + 1) * LANES)

    def chunk_in(c):
        at = pl.ds(c * chunk, chunk)
        to = pl.ds(1 + c * chunk, chunk)
        copies = [pltpu.make_async_copy(state.at[0, at], dens.at[to], in_sems.at[c, 0])]
        for f in range(6):
            copies.append(
                pltpu.make_async_copy(state.at[f + 2, at], flds.at[f, to], in_sems.at[c, f + 1])
            )
        return copies

    def rows_in(source, side):
        to = 0 if side == 0 else nx + 1
        copies = [
            pltpu.make_async_copy(source.at[0], dens.at[to], halo_sems.at[side, 0]),
            pltpu.make_async_copy(source.at[pl.ds(2, 6)], flds.at[:, to], halo_sems.at[side, 1]),
        ]
        if side == 1:
            copies.append(
                pltpu.make_async_copy(source.at[8], flds.at[3, nx + 2], halo_sems.at[side, 2])
            )
        return copies

    def cols_in(source, side):
        return [pltpu.make_async_copy(source, rims.at[side, :, pl.ds(8, nx)], halo_sems.at[side, 3])]

    def corner_in(source, half, side, end):
        to = pl.ds(0 if end == 0 else nx + 8, 8)
        return [
            pltpu.make_async_copy(source.at[half], rims.at[side, :, to], halo_sems.at[side, 4 + end])
        ]

    for side in range(2):
        @pl.when(row_par == side)
        def _():
            for c in rows_in(row_odd, side):
                c.start()

        @pl.when(row_par != side)
        def _():
            for c in rows_in(row_even, side):
                c.start()

        @pl.when(col_par == side)
        def _():
            for c in cols_in(col_odd, side):
                c.start()

        @pl.when(col_par != side)
        def _():
            for c in cols_in(col_even, side):
                c.start()

        half = jnp.where(col_par == side, 1, 0)
        for end in range(2):
            @pl.when(row_par == end)
            def _():
                for c in corner_in(cor_odd, half, side, end):
                    c.start()

            @pl.when(row_par != end)
            def _():
                for c in corner_in(cor_even, half, side, end):
                    c.start()

    for c in range(ahead):
        for copy in chunk_in(c):
            copy.start()

    for side in range(2):
        for c in rows_in(row_even, side) + cols_in(col_even, side):
            c.wait()
        for end in range(2):
            for c in corner_in(cor_even, 0, side, end):
                c.wait()

    for at in (0, nx + 1):
        dens[at] = jnp.where(dens[at] > 0.0, dens[at], 1.0)

    span = rims.shape[2]
    rim_lane = lax.broadcasted_iota(jnp.int32, (span, LANES), 1)
    for side in range(2):
        face_z = [rims[side, 7, :, cut(k)] for k in range(nk)]
        face_z_up = lane_up(face_z, rim_lane)
        for k in range(nk):
            rho = rims[side, 0, :, cut(k)]
            inv = scaled_inverse(jnp.where(rho > 0.0, rho, 1.0))
            vel_x = rims[side, 2, :, cut(k)] * inv
            vel_y = rims[side, 3, :, cut(k)] * inv
            vel_z = rims[side, 4, :, cut(k)] * inv
            face_x = rims[side, 5, :, cut(k)]
            mag_x = face_x + pltpu.roll(face_x, span - 1, 0)
            mag_z = face_z[k] + face_z_up[k]
            mag_y = rims[side, 6, :, cut(k)]
            if side == 1:
                rim_e[3, 0, k] = mag_y
                mag_y = mag_y + rims[side, 8, :, cut(k)]
            rim_e[side, 0, k] = vel_y * mag_x - vel_x * mag_y
            rim_e[side, 1, k] = vel_z * mag_y - vel_y * mag_z
            if side == 0:
                rim_e[2, 0, k] = vel_x
                rim_e[2, 1, k] = vel_z

    prev[...] = jnp.zeros_like(prev)
    lane = lax.broadcasted_iota(jnp.int32, (8, LANES), 1)
    row = lax.broadcasted_iota(jnp.int32, (8, LANES), 0)
    zero = jnp.zeros((8, LANES), F32)
    nj = ny // 8

    def up_of(value):
        rolled = functools.cache(
            lambda k: pltpu.roll(value(k), LANES - 1, 1) if k < nk else zero
        )
        return lambda k: jnp.where(lane == LANES - 1, rolled(k + 1), rolled(k))

    def down_of(value):
        rolled = functools.cache(lambda k: pltpu.roll(value(k), 1, 1) if k >= 0 else zero)
        return lambda k: jnp.where(lane == 0, rolled(k - 1), rolled(k))

    def plane(p, carry):
        @pl.when((p % chunk == 0) & (p < nx))
        def _():
            for copy in chunk_in(p // chunk):
                copy.wait()

        @pl.when((p % chunk == 0) & (p < nx - ahead * chunk))
        def _():
            for copy in chunk_in(p // chunk + ahead):
                copy.start()

        at_rim = pl.ds(p + 7, 1)
        for k in range(nk):
            first = flds[4, p, 0:1, cut(k)]
            edge[0, k, 7:8] = rim_e[0, 0, k, at_rim] - rim_e[2, 0, k, at_rim] * first
            edge[1, k, 7:8] = rim_e[0, 1, k, at_rim] + rim_e[2, 1, k, at_rim] * first
            edge[0, k, ny + 8 : ny + 9] = rim_e[1, 0, k, at_rim]
            edge[1, k, ny + 8 : ny + 9] = rim_e[1, 1, k, at_rim]
        for j in range(nj):
            at = slice(8 * j, 8 * j + 8)
            to = slice(8 * j + 8, 8 * j + 16)
            face_z = functools.cache(lambda k: flds[5, p, at, cut(k)])
            face_z_up = up_of(face_z)
            for k in range(nk):
                inv = scaled_inverse(dens[p, at, cut(k)])
                vel_x = flds[0, p, at, cut(k)] * inv
                vel_y = flds[1, p, at, cut(k)] * inv
                vel_z = flds[2, p, at, cut(k)] * inv
                face_y = flds[4, p, at, cut(k)]
                mag_x = flds[3, p, at, cut(k)] + flds[3, p + 1, at, cut(k)]
                if j < nj - 1:
                    after = flds[4, p, 8 * j + 8 : 8 * j + 9, cut(k)]
                else:
                    after = rim_e[3, 0, k, at_rim]
                mag_y = face_y + jnp.where(row == 7, after, pltpu.roll(face_y, 7, 0))
                mag_z = face_z(k) + face_z_up(k)
                edge[0, k, to] = vel_y * mag_x - vel_x * mag_y
                edge[1, k, to] = vel_z * mag_y - vel_y * mag_z
                edge[2, k, to] = vel_x * mag_z - vel_z * mag_x
        before = jnp.maximum(p - 1, 0)
        for j in range(nj):
            at = slice(8 * j, 8 * j + 8)
            low, mid, high = (slice(8 * j + n, 8 * j + n + 8) for n in (7, 8, 9))
            elec_y = functools.cache(lambda k: edge[2, k, mid])
            x_sum = functools.cache(lambda k: edge[1, k, low] + edge[1, k, mid])
            x_diff = functools.cache(lambda k: edge[1, k, high] - edge[1, k, low])
            y_down, y_up = down_of(elec_y), up_of(elec_y)
            sum_down, sum_up = down_of(x_sum), up_of(x_sum)
            diff_down = down_of(x_diff)
            for k in range(nk):
                z_low = edge[0, k, low]
                below = y_down(k)
                turn = (edge[0, k, high] - z_low) - (y_up(k) - below)
                z_sum = z_low + edge[0, k, mid]
                y_sum = below + elec_y(k)
                done[0, p, at, cut(k)] = flds[3, p, at, cut(k)] - (prev[0, k, at] + turn)
                done[1, before, at, cut(k)] = prev[3, k, at] + z_sum
                done[2, before, at, cut(k)] = prev[4, k, at] - y_sum
                prev[3, k, at] = (flds[4, p, at, cut(k)] - prev[1, k, at]) - (
                    sum_up(k) - sum_down(k)
                )
                prev[4, k, at] = (flds[5, p, at, cut(k)] + prev[2, k, at]) + (
                    diff_down(k) + x_diff(k)
                )
                prev[0, k, at] = turn
                prev[1, k, at] = z_sum
                prev[2, k, at] = y_sum

        @pl.when((p > chunk) & ((p - 1) % chunk == 0))
        def _():
            chunk_out((p - 1) // chunk - 1).start()

        return carry

    def chunk_out(c):
        return pltpu.make_async_copy(
            done.at[:, pl.ds(1 + c * chunk, chunk)],
            out.at[:, pl.ds(c * chunk, chunk)],
            out_sems.at[c],
        )

    lax.fori_loop(0, nx + 2, plane, 0)
    for c in range(chunks):
        chunk_out(c).wait()


def advance(state, rows_halo, cols_halo, corners):
    nx, ny, nz = state.shape[1:]
    nk = nz // LANES
    return pl.pallas_call(
        advance_kernel,
        out_shape=jax.ShapeDtypeStruct((3, nx, ny, nz), F32),
        in_specs=[ANY] * 7,
        out_specs=ANY,
        scratch_shapes=[
            pltpu.VMEM((nx + 2, ny, nz), F32),
            pltpu.VMEM((6, nx + 3, ny, nz), F32),
            pltpu.VMEM((2, 9, nx + 16, nz), F32),
            pltpu.VMEM((4, 2, nk, nx + 16, LANES), F32),
            pltpu.VMEM((3, nk, ny + 16, LANES), F32),
            pltpu.VMEM((5, nk, ny, LANES), F32),
            pltpu.VMEM((3, nx + 2, ny, nz), F32),
            pltpu.SemaphoreType.DMA((nx // 4, 7)),
            pltpu.SemaphoreType.DMA((2, 6)),
            pltpu.SemaphoreType.DMA((nx // 4,)),
        ],
        compiler_params=pltpu.CompilerParams(vmem_limit_bytes=50 * MIB),
        cost_estimate=pl.CostEstimate(
            flops=60 * nx * ny * nz, bytes_accessed=40 * nx * ny * nz, transcendentals=0
        ),
        name="advance",
    )(state, *rows_halo, *cols_halo, *corners)


SIDE = BS // 2 + 2
WIDE = BS + 2


PITCH = (WIDE + 1) * 24


def z_place(kz, nk):
    begin = kz * BS - 1
    tile = (begin + LANES) // LANES - 1
    columns = [
        pl.ds(pl.multiple_of(jnp.clip(tile + t, 0, nk - 1) * LANES, LANES), LANES)
        for t in range(2)
    ]
    return columns, begin - tile * LANES


ROWS = 56
X_ROWS, Y_ROWS, Z_ROWS = slice(32, 40), slice(40, 48), slice(48, 56)


def turned(value, amount):
    return pltpu.roll(value, amount % LANES, 1) if amount % LANES else value


def to_lane(value, amount):
    return pltpu.roll(value, lax.rem(amount + 2 * LANES, LANES), 1)


def lanes_from(lane, first, count):
    first = first % LANES
    return (lane >= first) & (lane < first + count)


def put_z(lane, side, low, high, half, quarter, c):
    at = lane % 8
    here = (lane >= 64) if half else (lane < 64)
    low = turned(low, 64 * half + 2 * quarter + 1 - 8 * c)
    high = turned(high, 64 * half + 2 * quarter - 7 - 8 * c)
    side = jnp.where(here & (at == 2 * quarter), low, side)
    return jnp.where(here & (at == 2 * quarter + 1), high, side)


def own_kernel(state, flags, owners, out, info, window, aligned, sems):
    nx, ny, nz = state.shape[1:]
    nk = nz // LANES
    gx, gy, gz = flags.shape
    grid = (gy, gz)
    number = lax.broadcasted_iota(jnp.int32, grid, 0) * gz + lax.broadcasted_iota(
        jnp.int32, grid, 1
    )
    first = jnp.full(grid, gx * gy * gz - 1, jnp.int32)
    last = jnp.zeros(grid, jnp.int32)
    for x in range(gx):
        flagged = flags[x] == 1
        here = number + x * gy * gz
        first = jnp.minimum(first, jnp.where(flagged, here, gx * gy * gz - 1))
        last = jnp.maximum(last, jnp.where(flagged, here, 0))
    found = (
        jnp.min(first.astype(F32)).astype(jnp.int32),
        jnp.max(last.astype(F32)).astype(jnp.int32),
    )
    spots = []
    for r in range(PARENTS):
        ix, iy, kz = found[r] // (gy * gz), found[r] // gz % gy, found[r] % gz
        columns, shift = z_place(kz, nk)
        y_from = pl.multiple_of(8 * iy, 8)
        copies = []
        for f in range(8):
            for t in range(2):
                copies.append(
                    pltpu.make_async_copy(
                        state.at[f, pl.ds((BS - 1) * ix, BS + 1), pl.ds(y_from, 24), columns[t]],
                        window.at[r, t, f],
                        sems.at[r, t, f],
                    )
                )
        if r == 0:
            for c in copies:
                c.start()
        spots.append((ix, iy, kz, shift, copies))
        info[3 * r], info[3 * r + 1], info[3 * r + 2] = ix, iy, kz

    names = [owners[n, 0] for n in range(KIDS)]
    for n in range(KIDS):
        rank = jnp.int32(0)
        for m in range(n):
            rank = rank + jnp.where(names[m] == names[n], 1, 0)
        info[3 * PARENTS + n] = names[n] * CAP + rank

    lane = lax.broadcasted_iota(jnp.int32, (8, LANES), 1)
    zero = jnp.zeros((8, LANES), F32)
    for r in range(PARENTS):
        ix, iy, kz, shift, copies = spots[r]
        for c in copies:
            c.wait()
        if r + 1 < PARENTS:
            for c in spots[r + 1][4]:
                c.start()
        from_first = lane >= shift
        outside = ((kz == 0) & (lane == shift)) | (
            (kz == nz // BS - 1) & (lane == lax.rem(shift + WIDE - 1, LANES))
        )

        def align(i, carry):
            for f in range(8):
                for y in range(3):
                    rows = slice(8 * y, 8 * y + 8)
                    value = jnp.where(
                        from_first, window[r, 0, f, i, rows], window[r, 1, f, i, rows]
                    )
                    value = jnp.where(outside, 1.0 if f == 0 else 0.0, value)
                    at = pl.multiple_of(f * PITCH + i * 24 + 8 * y, 8)
                    aligned[pl.ds(at, 8)] = value
            return carry

        lax.fori_loop(0, BS + 1, align, 0, unroll=True)

        def pair(number, carry):
            low_x, low_y = number // 2, number % 2
            plane_at = 8 * low_x - 1 + ix
            row_at = 8 * low_y - 1 + 8 * iy
            sums = None
            y_side = [zero, zero]
            z_side = [zero, zero]
            x_side = [zero, zero]
            held = None
            for i in range(SIDE):
                plane = jnp.clip(plane_at + i, 0, BS)
                sums = [zero, zero]
                z_low = [zero, zero]
                z_high = [zero, zero]
                inner = 0 < i < SIDE - 1
                for j in range(SIDE):
                    if not inner and not 0 < j < SIDE - 1:
                        continue
                    base = plane * 24 + jnp.clip(row_at + j, 0, 23)
                    value = aligned[pl.ds(base, 8, stride=PITCH), :]
                    if 0 < j < SIDE - 1:
                        moved = to_lane(value, 8 * (j - 1) - 1 - shift)
                        for c in range(2):
                            first = 8 * (j - 1) + 8 * c
                            sums[c] = jnp.where(lanes_from(lane, first, 8), moved, sums[c])
                            if inner:
                                z_low[c] = jnp.where(
                                    lanes_from(lane, first - 1, 1), moved, z_low[c]
                                )
                                z_high[c] = jnp.where(
                                    lanes_from(lane, first + 8, 1), moved, z_high[c]
                                )
                    else:
                        half, quarter = (i - 1) % 2, (i - 1) // 2
                        first = 64 * half + 16 * quarter + (8 if j else 0)
                        moved = to_lane(value, first - 1 - shift)
                        for c in range(2):
                            y_side[c] = jnp.where(
                                lanes_from(lane, first + 8 * c, 8), moved, y_side[c]
                            )
                for c in range(2):
                    child = 8 * r + 2 * number + c
                    if inner:
                        half, quarter = (i - 1) % 2, (i - 1) // 2
                        z_side[c] = put_z(lane, z_side[c], z_low[c], z_high[c], half, quarter, c)
                        if half:
                            out[child, 8 * quarter : 8 * quarter + 8] = jnp.where(
                                lane < 64, turned(held[c], -8 * c), turned(sums[c], 64 - 8 * c)
                            )
                    elif i:
                        x_side[c] = jnp.where(lane < 64, turned(sums[c], -8 * c), x_side[c])
                    else:
                        x_side[c] = turned(sums[c], 64 - 8 * c)
                held = sums
            for c in range(2):
                child = 8 * r + 2 * number + c
                out[child, X_ROWS] = x_side[c]
                out[child, Y_ROWS] = turned(y_side[c], -8 * c)
                out[child, Z_ROWS] = z_side[c]
            return carry

        lax.fori_loop(0, 4, pair, 0)


def own_pieces(state, flags, owners):
    fields = state.shape[0]
    return pl.pallas_call(
        own_kernel,
        out_shape=[
            jax.ShapeDtypeStruct((KIDS, ROWS, LANES), F32),
            jax.ShapeDtypeStruct((3 * PARENTS + KIDS,), jnp.int32),
        ],
        in_specs=[ANY, pl.BlockSpec(memory_space=pltpu.VMEM), SMEM],
        out_specs=[pl.BlockSpec(memory_space=pltpu.VMEM), SMEM],
        scratch_shapes=[
            pltpu.VMEM((PARENTS, 2, fields, BS + 1, 24, LANES), F32),
            pltpu.VMEM((fields * PITCH, LANES), F32),
            pltpu.SemaphoreType.DMA((PARENTS, 2, fields)),
        ],
        compiler_params=pltpu.CompilerParams(vmem_limit_bytes=50 * MIB),
        cost_estimate=pl.CostEstimate(
            flops=10**7, bytes_accessed=20 * 10**6, transcendentals=0
        ),
        name="own_pieces",
    )(state, flags, owners)


def corner_kernel(col_even, col_odd, cor_even, cor_odd, sems):
    nx = col_even.shape[1]
    high_in_even = parity("rows") == 0
    copies = []
    for number, (ref, high) in enumerate(
        ((cor_even, high_in_even), (cor_odd, jnp.logical_not(high_in_even)))
    ):
        at = pl.ds(pl.multiple_of(jnp.where(high, nx - 8, 0), 8), 8)
        for half, source in enumerate((col_even, col_odd)):
            copies.append(
                pltpu.make_async_copy(source.at[:, at], ref.at[half], sems.at[number, half])
            )
    for c in copies:
        c.start()
    for c in copies:
        c.wait()


def pack_corners(col_even, col_odd):
    layers, _, nz = col_even.shape
    corner = jax.ShapeDtypeStruct((2, layers, 8, nz), F32)
    return pl.pallas_call(
        corner_kernel,
        out_shape=[corner, corner],
        in_specs=[ANY] * 2,
        out_specs=[pl.BlockSpec(memory_space=pltpu.VMEM)] * 2,
        scratch_shapes=[pltpu.SemaphoreType.DMA((2, 2))],
        compiler_params=pltpu.CompilerParams(vmem_limit_bytes=8 * MIB),
        name="pack_corners",
    )(col_even, col_odd)


def finish_kernel(
    info, own, row_even, row_odd, col_even, col_odd, out, beside_x, beside_y, kid_sems, sems
):
    nk = row_even.shape[2] // LANES
    nx = col_even.shape[1]
    row_par, col_par = parity("rows"), parity("cols")
    waits = []
    for r in range(PARENTS):
        ix, iy, kz = info[3 * r], info[3 * r + 1], info[3 * r + 2]
        columns, shift = z_place(kz, nk)
        for t in range(2):

            def row_copy(source):
                return pltpu.make_async_copy(
                    source.at[pl.ds(0, 8), pl.ds(pl.multiple_of(iy * BS, BS), BS), columns[t]],
                    beside_x.at[r, t],
                    sems.at[r, t, 0],
                )

            def col_copy(source):
                return pltpu.make_async_copy(
                    source.at[pl.ds(0, 8), pl.ds(pl.multiple_of(ix * BS, BS), BS), columns[t]],
                    beside_y.at[r, t],
                    sems.at[r, t, 1],
                )

            @pl.when(ix != row_par)
            def _():
                row_copy(row_even).start()

            @pl.when(ix == row_par)
            def _():
                row_copy(row_odd).start()

            @pl.when(iy != col_par)
            def _():
                col_copy(col_even).start()

            @pl.when(iy == col_par)
            def _():
                col_copy(col_odd).start()

            waits += [row_copy(row_even), col_copy(col_even)]
    out[...] = jnp.zeros_like(out)
    kid_copies = [
        pltpu.make_async_copy(own.at[n], out.at[info[3 * PARENTS + n]], kid_sems.at[n])
        for n in range(KIDS)
    ]
    for c in kid_copies:
        c.start()
    for c in waits + kid_copies:
        c.wait()

    lane = lax.broadcasted_iota(jnp.int32, (8, LANES), 1)
    sub = lax.broadcasted_iota(jnp.int32, (8, LANES), 0)
    zero = jnp.zeros((8, LANES), F32)
    for r in range(PARENTS):
        ix, iy, kz = info[3 * r], info[3 * r + 1], info[3 * r + 2]
        _, shift = z_place(kz, nk)
        from_first = lane >= shift

        def cell(source, n):
            halves = [flat_rows(source.at[r, t])[pl.ds(n, 8, stride=BS), :] for t in range(2)]
            value = jnp.where(from_first, halves[0], halves[1])
            return jnp.where((sub == 0) & (value == 0.0), 1.0, value)

        first_kid = 3 * PARENTS + 8 * r
        here = (lane < 64) == (ix == 1)
        for b in range(2):
            sums = [zero, zero]
            for j in range(8):
                moved = to_lane(cell(beside_x, 8 * b + j), 8 * j - 1 - shift)
                for c in range(2):
                    sums[c] = jnp.where(lanes_from(lane, 8 * j + 8 * c, 8), moved, sums[c])
            for c in range(2):
                slot = info[first_kid + 4 * ix + 2 * b + c]
                value = to_lane(sums[c], 64 * (1 - ix) - 8 * c)
                out[slot, X_ROWS] = jnp.where(here, value, out[slot, X_ROWS])

        here = (lane // 8) % 2 == iy
        for a in range(2):
            sums = [zero, zero]
            for i in range(8):
                first = 64 * (i % 2) + 16 * (i // 2)
                moved = to_lane(cell(beside_y, 8 * a + i), first - 1 - shift)
                for c in range(2):
                    sums[c] = jnp.where(lanes_from(lane, first + 8 * c, 8), moved, sums[c])
            for c in range(2):
                slot = info[first_kid + 4 * a + 2 * iy + c]
                value = to_lane(sums[c], 8 * iy - 8 * c)
                out[slot, Y_ROWS] = jnp.where(here, value, out[slot, Y_ROWS])


def finish_pieces(info, own, rows_halo, cols_halo, count):
    return pl.pallas_call(
        finish_kernel,
        out_shape=jax.ShapeDtypeStruct((count * CAP, ROWS, LANES), F32),
        in_specs=[SMEM] + [ANY] * 5,
        out_specs=pl.BlockSpec(memory_space=pltpu.VMEM),
        scratch_shapes=[
            pltpu.VMEM((PARENTS, 2, 8, BS, LANES), F32),
            pltpu.VMEM((PARENTS, 2, 8, BS, LANES), F32),
            pltpu.SemaphoreType.DMA((KIDS,)),
            pltpu.SemaphoreType.DMA((PARENTS, 2, 2)),
        ],
        compiler_params=pltpu.CompilerParams(vmem_limit_bytes=8 * MIB),
        name="finish_pieces",
    )(info, own, *rows_halo, *cols_halo)


def spread_weights():
    spread = np.zeros((3, LANES, 512), np.float32)
    for half in range(2):
        for y in range(BS):
            for z in range(BS):
                at = half * 64 + y // 2 * 8 + z // 2
                to = half * 256 + y * BS + z
                spread[0, at, to] = 1.0
                spread[1, at, to] = 0.25 * (2 * (y % 2) - 1)
                spread[2, at, to] = 0.25 * (2 * (z % 2) - 1)
    return spread


def limited(left, right):
    return jnp.maximum(jnp.minimum(left, right), 0.0) + jnp.minimum(jnp.maximum(left, right), 0.0)


def halves_of(value):
    top = value.astype(BF16)
    return top, (value - top.astype(F32)).astype(BF16)


def prolong_kernel(weights, piece, out, staged):
    count = piece.shape[0]
    sub = lax.broadcasted_iota(jnp.int32, (8, LANES), 0)
    lane = lax.broadcasted_iota(jnp.int32, (8, LANES), 1)
    cells = sub < 5

    def slopes(s, carry):
        for q in range(4):
            one_set(s, q)
        return carry

    def one_set(s, q):
        here = piece[s, 8 * q : 8 * q + 8]
        after = piece[s, 8 * q + 8 : 8 * q + 16] if q < 3 else piece[s, X_ROWS]
        prior = piece[s, 8 * q - 8 : 8 * q] if q else piece[s, X_ROWS]
        rows, points = piece[s, Y_ROWS], piece[s, Z_ROWS]
        x_up = turned(jnp.where(lane < 64, after, here), 64) - here
        x_down = here - turned(jnp.where(lane < 64, here, prior), 64)
        y_up = jnp.where(lane % 64 >= 56, turned(rows, 48 - 16 * q), turned(here, -8)) - here
        y_down = here - jnp.where(lane % 64 < 8, turned(rows, -16 * q), turned(here, 8))
        z_up = jnp.where(lane % 8 == 7, turned(points, 6 - 2 * q), turned(here, -1)) - here
        z_down = here - jnp.where(lane % 8 == 0, turned(points, -2 * q), turned(here, 1))
        slope_x = jnp.where(cells, limited(x_up, x_down), jnp.where(sub == 5, x_up, 0.0))
        slope_y = jnp.where(cells, limited(y_up, y_down), jnp.where(sub == 6, y_up, 0.0))
        slope_z = jnp.where(cells, limited(z_up, z_down), jnp.where(sub == 7, z_up, 0.0))
        middle = here + jnp.where(cells, 0.0, 0.25 * (slope_x + slope_y + slope_z))
        at = pl.ds(pl.multiple_of(s * 32, 32) + 8 * q, 8)
        step = 0.25 * slope_x
        staged[0, at] = middle - step
        staged[1, at] = middle + step
        staged[2, at] = slope_y
        staged[3, at] = slope_z

    lax.fori_loop(0, count, slopes, 0)

    def dot(parts, matrix):
        halves = [halves_of(staged[n]) for n in parts]
        value = jnp.concatenate([h[0] for h in halves] + [h[1] for h in halves], axis=1)
        return jnp.dot(value, matrix, preferred_element_type=F32)

    tilt = dot((2, 3), weights[2 * LANES :])
    for p in range(2):
        fine = dot((p,), weights[0 : 2 * LANES]) + tilt
        for s in range(count):
            for i in range(8):
                x = 2 * i + p
                at = s * 32 + 8 * (i // 2)
                out[0, 0, s // 2, s % 2, :, x * 256 : (x + 1) * 256] = fine[
                    at : at + 8, 256 * (i % 2) : 256 * (i % 2) + 256
                ]


def prolong(received, count):
    group = 8
    weights = spread_weights()
    stacked = np.concatenate([weights[n] for n in (0, 0, 1, 2, 1, 2)])
    return pl.pallas_call(
        prolong_kernel,
        grid=(count * CAP // group,),
        out_shape=jax.ShapeDtypeStruct((1, 1, count, CAP, 8, BS**3), F32),
        in_specs=[
            pl.BlockSpec(stacked.shape, lambda g: (0, 0)),
            pl.BlockSpec((group, ROWS, LANES), lambda g: (g, 0, 0)),
        ],
        out_specs=pl.BlockSpec(
            (1, 1, group // CAP, CAP, 8, BS**3), lambda g: (0, 0, g, 0, 0, 0)
        ),
        scratch_shapes=[pltpu.VMEM((4, group * 32, LANES), F32)],
        compiler_params=pltpu.CompilerParams(vmem_limit_bytes=16 * MIB),
        name="prolong",
    )(jnp.asarray(stacked, BF16), received)


def on_device(state, flags, owners):
    rows, cols = lax.axis_size("rows"), lax.axis_size("cols")
    row_even, row_odd, col_even, col_odd = pack(state)
    col_even = lax.ppermute(col_even, "cols", even_swap(cols))
    col_odd = lax.ppermute(col_odd, "cols", odd_swap(cols))
    row_even = lax.ppermute(row_even, "rows", even_swap(rows))
    row_odd = lax.ppermute(row_odd, "rows", odd_swap(rows))
    own, info = own_pieces(state, flags, owners)
    own, row_even, row_odd, col_even, col_odd = lax.optimization_barrier(
        (own, row_even, row_odd, col_even, col_odd)
    )
    rows_halo, cols_halo = (row_even, row_odd), (col_even, col_odd)
    cor_even, cor_odd = pack_corners(col_even, col_odd)
    cor_even = lax.ppermute(cor_even, "rows", even_swap(rows))
    cor_odd = lax.ppermute(cor_odd, "rows", odd_swap(rows))
    sent = finish_pieces(info, own, rows_halo, cols_halo, cols)
    sent, cor_even, cor_odd = lax.optimization_barrier((sent, cor_even, cor_odd))
    received = lax.all_to_all(
        sent.reshape((cols, CAP) + sent.shape[1:]), "cols", split_axis=0, concat_axis=0, tiled=True
    )
    faces_new = advance(state, rows_halo, cols_halo, (cor_even, cor_odd))
    arrivals = prolong(received.reshape(sent.shape), cols)
    return faces_new, arrivals


def solution(mesh):
    return jax.shard_map(
        on_device,
        mesh=mesh,
        in_specs=(
            P(None, "rows", "cols", None),
            P("rows", "cols", None),
            P(("rows", "cols"), None),
        ),
        out_specs=(P(None, "rows", "cols", None), P("rows", "cols", None, None, None, None)),
        check_vma=False,
    )
```

```python
import functools

import jax
import jax.numpy as jnp
import numpy as np
from jax import lax
from jax.experimental import pallas as pl
from jax.experimental.pallas import tpu as pltpu
from jax.sharding import PartitionSpec as P

F32 = jnp.float32
BF16 = jnp.bfloat16
BS = 16
CAP = 2
PARENTS = 2
KIDS = 16
LANES = 128
MIB = 1024 * 1024
ANY = pl.BlockSpec(memory_space=pl.ANY)
SMEM = pl.BlockSpec(memory_space=pltpu.SMEM)

courant = 0.3
SCALE = 0.25 * 0.5 * courant


def even_swap(count):
    return [(i, i ^ 1) for i in range(count)]


def odd_swap(count):
    return [p for i in range(1, count - 1, 2) for p in ((i, i + 1), (i + 1, i))]


def flat_rows(ref):
    rows = 1
    for n in ref.shape[:-1]:
        rows *= n
    return ref.reshape(rows, ref.shape[-1])


def parity(axis):
    return lax.rem(lax.axis_index(axis), 2)


def pack_kernel(state, col_even, col_odd, token, tiles, rims, sems, out_sems):
    nx, ny = state.shape[1], state.shape[2]
    nk = state.shape[3] // LANES

    def tile_in(side, k, f):
        return pltpu.make_async_copy(
            state.at[pl.ds(f, 2), :, pl.ds(side * (ny - 8), 8), pl.ds(k * LANES, LANES)],
            tiles.at[side, k, pl.ds(f, 2)],
            sems.at[side, k, f],
        )

    for k in range(nk):
        for side in range(2):
            for f in range(0, 8, 2):
                tile_in(side, k, f).start()
    high_in_even = parity("cols") == 0
    outs = []
    for k in range(nk):
        for side in range(2):
            for f in range(0, 8, 2):
                tile_in(side, k, f).wait()
        low_tile = flat_rows(tiles.at[0, k])
        high_tile = flat_rows(tiles.at[1, k])
        for layer in range(9):
            field = layer if layer < 8 else 6
            at_low = field * nx * 8 + (0 if layer < 8 else 1)
            at_high = field * nx * 8 + (7 if layer < 8 else 6)
            low = low_tile[pl.ds(at_low, nx, stride=8), :]
            high = high_tile[pl.ds(at_high, nx, stride=8), :]
            rims[0, k, layer] = jnp.where(high_in_even, high, low)
            rims[1, k, layer] = jnp.where(high_in_even, low, high)
        for number, ref in enumerate((col_even, col_odd)):
            c = pltpu.make_async_copy(
                rims.at[number, k],
                ref.at[:, :, pl.ds(k * LANES, LANES)],
                out_sems.at[number, k],
            )
            c.start()
            outs.append(c)
    token[0] = 0
    for c in outs:
        c.wait()


def pack(state):
    fields, nx, ny, nz = state.shape
    nk = nz // LANES
    col_shape = jax.ShapeDtypeStruct((fields + 1, nx, nz), F32)
    return pl.pallas_call(
        pack_kernel,
        out_shape=[col_shape, col_shape, jax.ShapeDtypeStruct((1,), jnp.int32)],
        in_specs=[ANY],
        out_specs=[ANY, ANY, SMEM],
        scratch_shapes=[
            pltpu.VMEM((2, nk, fields, nx, 8, LANES), F32),
            pltpu.VMEM((2, nk, fields + 1, nx, LANES), F32),
            pltpu.SemaphoreType.DMA((2, nk, fields)),
            pltpu.SemaphoreType.DMA((2, nk)),
        ],
        compiler_params=pltpu.CompilerParams(vmem_limit_bytes=50 * MIB),
        name="pack",
    )(state)


def lane_up(parts, lane):
    rolled = [pltpu.roll(p, LANES - 1, 1) for p in parts]
    rolled.append(jnp.zeros_like(parts[0]))
    return [jnp.where(lane == LANES - 1, rolled[k + 1], rolled[k]) for k in range(len(parts))]


def lane_down(parts, lane):
    rolled = [pltpu.roll(p, 1, 1) for p in parts]
    rolled = [jnp.zeros_like(parts[0])] + rolled
    return [jnp.where(lane == 0, rolled[k], rolled[k + 1]) for k in range(len(parts))]


def scaled_inverse(rho):
    guess = pl.reciprocal(rho, approx=True)
    guess = guess * (2.0 - rho * guess)
    guess = guess * (2.0 - rho * guess)
    return SCALE * guess


def advance_kernel(
    state, row_even, row_odd, col_even, col_odd, cor_even, cor_odd,
    out, dens, flds, rims, ends, rim_e, edge, prev, done, in_sems, halo_sems, out_sems,
):
    nx, ny, nz = state.shape[1:]
    nk = nz // LANES
    chunk = 4
    chunks = nx // chunk
    ahead = 3
    row_par, col_par = parity("rows"), parity("cols")

    def cut(k):
        return slice(k * LANES, (k + 1) * LANES)

    def chunk_in(c):
        at = pl.ds(c * chunk, chunk)
        to = pl.ds(1 + c * chunk, chunk)
        copies = [pltpu.make_async_copy(state.at[0, at], dens.at[to], in_sems.at[c, 0])]
        for f in range(6):
            copies.append(
                pltpu.make_async_copy(state.at[f + 2, at], flds.at[f, to], in_sems.at[c, f + 1])
            )
        return copies

    def rows_in(source, side):
        to = 0 if side == 0 else nx + 1
        copies = [
            pltpu.make_async_copy(source.at[0], dens.at[to], halo_sems.at[side, 0]),
            pltpu.make_async_copy(source.at[pl.ds(2, 6)], flds.at[:, to], halo_sems.at[side, 1]),
        ]
        if side == 1:
            copies.append(
                pltpu.make_async_copy(source.at[8], flds.at[3, nx + 2], halo_sems.at[side, 2])
            )
        return copies

    def cols_in(source, side):
        return [pltpu.make_async_copy(source, rims.at[side, :, pl.ds(8, nx)], halo_sems.at[side, 3])]

    corner_copies = [
        pltpu.make_async_copy(source, ends.at[n], halo_sems.at[n, 4])
        for n, source in enumerate((cor_even, cor_odd))
    ]
    for c in corner_copies:
        c.start()

    for side in range(2):
        @pl.when(row_par == side)
        def _():
            for c in rows_in(row_odd, side):
                c.start()

        @pl.when(row_par != side)
        def _():
            for c in rows_in(row_even, side):
                c.start()

        @pl.when(col_par == side)
        def _():
            for c in cols_in(col_odd, side):
                c.start()

        @pl.when(col_par != side)
        def _():
            for c in cols_in(col_even, side):
                c.start()

    for c in range(ahead):
        for copy in chunk_in(c):
            copy.start()

    for side in range(2):
        for c in rows_in(row_even, side) + cols_in(col_even, side):
            c.wait()

    for c in corner_copies:
        c.wait()
    for side in range(2):
        for end in range(2):
            row_swap = jnp.where(row_par == end, 1, 0)
            col_swap = jnp.where(col_par == side, 1, 0)
            at = 7 if end == 0 else nx + 8
            for f in range(8):
                rims[side, f, at : at + 1] = ends[row_swap, col_swap, f : f + 1]
            rims[side, 8, at : at + 1] = ends[row_swap, col_swap, 9:10]
            if end == 1:
                rims[side, 5, at + 1 : at + 2] = ends[row_swap, col_swap, 8:9]

    for at in (0, nx + 1):
        dens[at] = jnp.where(dens[at] > 0.0, dens[at], 1.0)

    span = rims.shape[2]
    rim_lane = lax.broadcasted_iota(jnp.int32, (span, LANES), 1)
    for side in range(2):
        face_z = [rims[side, 7, :, cut(k)] for k in range(nk)]
        face_z_up = lane_up(face_z, rim_lane)
        for k in range(nk):
            rho = rims[side, 0, :, cut(k)]
            inv = scaled_inverse(jnp.where(rho > 0.0, rho, 1.0))
            vel_x = rims[side, 2, :, cut(k)] * inv
            vel_y = rims[side, 3, :, cut(k)] * inv
            vel_z = rims[side, 4, :, cut(k)] * inv
            face_x = rims[side, 5, :, cut(k)]
            mag_x = face_x + pltpu.roll(face_x, span - 1, 0)
            mag_z = face_z[k] + face_z_up[k]
            mag_y = rims[side, 6, :, cut(k)]
            if side == 1:
                rim_e[3, 0, k] = mag_y
                mag_y = mag_y + rims[side, 8, :, cut(k)]
            rim_e[side, 0, k] = vel_y * mag_x - vel_x * mag_y
            rim_e[side, 1, k] = vel_z * mag_y - vel_y * mag_z
            if side == 0:
                rim_e[2, 0, k] = vel_x
                rim_e[2, 1, k] = vel_z

    prev[...] = jnp.zeros_like(prev)
    lane = lax.broadcasted_iota(jnp.int32, (8, LANES), 1)
    row = lax.broadcasted_iota(jnp.int32, (8, LANES), 0)
    zero = jnp.zeros((8, LANES), F32)
    nj = ny // 8

    def up_of(value):
        rolled = functools.cache(
            lambda k: pltpu.roll(value(k), LANES - 1, 1) if k < nk else zero
        )
        return lambda k: jnp.where(lane == LANES - 1, rolled(k + 1), rolled(k))

    def down_of(value):
        rolled = functools.cache(lambda k: pltpu.roll(value(k), 1, 1) if k >= 0 else zero)
        return lambda k: jnp.where(lane == 0, rolled(k - 1), rolled(k))

    def plane(p, carry):
        @pl.when((p % chunk == 0) & (p < nx))
        def _():
            for copy in chunk_in(p // chunk):
                copy.wait()

        @pl.when((p % chunk == 0) & (p < nx - ahead * chunk))
        def _():
            for copy in chunk_in(p // chunk + ahead):
                copy.start()

        at_rim = pl.ds(p + 7, 1)
        for k in range(nk):
            first = flds[4, p, 0:1, cut(k)]
            edge[0, k, 7:8] = rim_e[0, 0, k, at_rim] - rim_e[2, 0, k, at_rim] * first
            edge[1, k, 7:8] = rim_e[0, 1, k, at_rim] + rim_e[2, 1, k, at_rim] * first
            edge[0, k, ny + 8 : ny + 9] = rim_e[1, 0, k, at_rim]
            edge[1, k, ny + 8 : ny + 9] = rim_e[1, 1, k, at_rim]
        for j in range(nj):
            at = slice(8 * j, 8 * j + 8)
            to = slice(8 * j + 8, 8 * j + 16)
            face_z = functools.cache(lambda k: flds[5, p, at, cut(k)])
            face_z_up = up_of(face_z)
            for k in range(nk):
                inv = scaled_inverse(dens[p, at, cut(k)])
                vel_x = flds[0, p, at, cut(k)] * inv
                vel_y = flds[1, p, at, cut(k)] * inv
                vel_z = flds[2, p, at, cut(k)] * inv
                face_y = flds[4, p, at, cut(k)]
                mag_x = flds[3, p, at, cut(k)] + flds[3, p + 1, at, cut(k)]
                if j < nj - 1:
                    after = flds[4, p, 8 * j + 8 : 8 * j + 9, cut(k)]
                else:
                    after = rim_e[3, 0, k, at_rim]
                mag_y = face_y + jnp.where(row == 7, after, pltpu.roll(face_y, 7, 0))
                mag_z = face_z(k) + face_z_up(k)
                edge[0, k, to] = vel_y * mag_x - vel_x * mag_y
                edge[1, k, to] = vel_z * mag_y - vel_y * mag_z
                edge[2, k, to] = vel_x * mag_z - vel_z * mag_x
        before = jnp.maximum(p - 1, 0)
        for j in range(nj):
            at = slice(8 * j, 8 * j + 8)
            low, mid, high = (slice(8 * j + n, 8 * j + n + 8) for n in (7, 8, 9))
            elec_y = functools.cache(lambda k: edge[2, k, mid])
            x_sum = functools.cache(lambda k: edge[1, k, low] + edge[1, k, mid])
            x_diff = functools.cache(lambda k: edge[1, k, high] - edge[1, k, low])
            y_down, y_up = down_of(elec_y), up_of(elec_y)
            sum_down, sum_up = down_of(x_sum), up_of(x_sum)
            diff_down = down_of(x_diff)
            for k in range(nk):
                z_low = edge[0, k, low]
                below = y_down(k)
                turn = (edge[0, k, high] - z_low) - (y_up(k) - below)
                z_sum = z_low + edge[0, k, mid]
                y_sum = below + elec_y(k)
                done[0, p, at, cut(k)] = flds[3, p, at, cut(k)] - (prev[0, k, at] + turn)
                done[1, before, at, cut(k)] = prev[3, k, at] + z_sum
                done[2, before, at, cut(k)] = prev[4, k, at] - y_sum
                prev[3, k, at] = (flds[4, p, at, cut(k)] - prev[1, k, at]) - (
                    sum_up(k) - sum_down(k)
                )
                prev[4, k, at] = (flds[5, p, at, cut(k)] + prev[2, k, at]) + (
                    diff_down(k) + x_diff(k)
                )
                prev[0, k, at] = turn
                prev[1, k, at] = z_sum
                prev[2, k, at] = y_sum

        @pl.when((p > chunk) & ((p - 1) % chunk == 0))
        def _():
            chunk_out((p - 1) // chunk - 1).start()

        return carry

    def chunk_out(c):
        return pltpu.make_async_copy(
            done.at[:, pl.ds(1 + c * chunk, chunk)],
            out.at[:, pl.ds(c * chunk, chunk)],
            out_sems.at[c],
        )

    lax.fori_loop(0, nx + 2, plane, 0)
    for c in range(chunks):
        chunk_out(c).wait()


def advance(state, rows_halo, cols_halo, corners):
    nx, ny, nz = state.shape[1:]
    nk = nz // LANES
    return pl.pallas_call(
        advance_kernel,
        out_shape=jax.ShapeDtypeStruct((3, nx, ny, nz), F32),
        in_specs=[ANY] * 7,
        out_specs=ANY,
        scratch_shapes=[
            pltpu.VMEM((nx + 2, ny, nz), F32),
            pltpu.VMEM((6, nx + 3, ny, nz), F32),
            pltpu.VMEM((2, 9, nx + 16, nz), F32),
            pltpu.VMEM((2, 2, 16, nz), F32),
            pltpu.VMEM((4, 2, nk, nx + 16, LANES), F32),
            pltpu.VMEM((3, nk, ny + 16, LANES), F32),
            pltpu.VMEM((5, nk, ny, LANES), F32),
            pltpu.VMEM((3, nx + 2, ny, nz), F32),
            pltpu.SemaphoreType.DMA((nx // 4, 7)),
            pltpu.SemaphoreType.DMA((2, 6)),
            pltpu.SemaphoreType.DMA((nx // 4,)),
        ],
        compiler_params=pltpu.CompilerParams(vmem_limit_bytes=50 * MIB),
        cost_estimate=pl.CostEstimate(
            flops=60 * nx * ny * nz, bytes_accessed=40 * nx * ny * nz, transcendentals=0
        ),
        name="advance",
    )(state, *rows_halo, *cols_halo, *corners)


SIDE = BS // 2 + 2
WIDE = BS + 2


PITCH = (WIDE + 1) * 24


def z_place(kz, nk):
    begin = kz * BS - 1
    tile = (begin + LANES) // LANES - 1
    columns = [
        pl.ds(pl.multiple_of(jnp.clip(tile + t, 0, nk - 1) * LANES, LANES), LANES)
        for t in range(2)
    ]
    return columns, begin - tile * LANES


ROWS = 56
X_ROWS, Y_ROWS, Z_ROWS = slice(32, 40), slice(40, 48), slice(48, 56)


def turned(value, amount):
    return pltpu.roll(value, amount % LANES, 1) if amount % LANES else value


def to_lane(value, amount):
    return pltpu.roll(value, lax.rem(amount + 2 * LANES, LANES), 1)


def lanes_from(lane, first, count):
    first = first % LANES
    return (lane >= first) & (lane < first + count)


def put_z(lane, side, low, high, half, quarter, c):
    at = lane % 8
    here = (lane >= 64) if half else (lane < 64)
    low = turned(low, 64 * half + 2 * quarter + 1 - 8 * c)
    high = turned(high, 64 * half + 2 * quarter - 7 - 8 * c)
    side = jnp.where(here & (at == 2 * quarter), low, side)
    return jnp.where(here & (at == 2 * quarter + 1), high, side)


def own_kernel(
    token, state, flags, owners, out, info, row_even, row_odd,
    window, aligned, sems, row_sems,
):
    nx, ny, nz = state.shape[1:]
    nk = nz // LANES
    gx, gy, gz = flags.shape
    grid = (gy, gz)
    number = lax.broadcasted_iota(jnp.int32, grid, 0) * gz + lax.broadcasted_iota(
        jnp.int32, grid, 1
    )
    first = jnp.full(grid, gx * gy * gz - 1, jnp.int32)
    last = jnp.zeros(grid, jnp.int32)
    for x in range(gx):
        flagged = flags[x] == 1
        here = number + x * gy * gz
        first = jnp.minimum(first, jnp.where(flagged, here, gx * gy * gz - 1))
        last = jnp.maximum(last, jnp.where(flagged, here, 0))
    found = (
        jnp.min(first.astype(F32)).astype(jnp.int32),
        jnp.max(last.astype(F32)).astype(jnp.int32),
    )
    spots = []
    for r in range(PARENTS):
        ix, iy, kz = found[r] // (gy * gz), found[r] // gz % gy, found[r] % gz
        columns, shift = z_place(kz, nk)
        y_from = pl.multiple_of(8 * iy, 8)
        copies = []
        for f in range(8):
            for t in range(2):
                copies.append(
                    pltpu.make_async_copy(
                        state.at[f, pl.ds((BS - 1) * ix, BS + 1), pl.ds(y_from, 24), columns[t]],
                        window.at[r, t, f],
                        sems.at[r, t, f],
                    )
                )
        if r == 0:
            for c in copies:
                c.start()
        spots.append((ix, iy, kz, shift, copies))
        info[3 * r], info[3 * r + 1], info[3 * r + 2] = ix, iy, kz

    at_even = jnp.where(parity("rows") == 0, nx - 1, 0)
    at_odd = nx - 1 - at_even
    row_copies = []
    for number, (ref, at) in enumerate(((row_even, at_even), (row_odd, at_odd))):
        second = jnp.where(at == 0, 1, nx - 2)
        row_copies.append(
            pltpu.make_async_copy(state.at[:, at], ref.at[pl.ds(0, 8)], row_sems.at[number, 0])
        )
        row_copies.append(
            pltpu.make_async_copy(state.at[5, second], ref.at[8], row_sems.at[number, 1])
        )
    for c in row_copies:
        c.start()

    names = [owners[n, 0] for n in range(KIDS)]
    for n in range(KIDS):
        rank = jnp.int32(0)
        for m in range(n):
            rank = rank + jnp.where(names[m] == names[n], 1, 0)
        info[3 * PARENTS + n] = names[n] * CAP + rank

    lane = lax.broadcasted_iota(jnp.int32, (8, LANES), 1)
    zero = jnp.zeros((8, LANES), F32)
    for r in range(PARENTS):
        ix, iy, kz, shift, copies = spots[r]
        for c in copies:
            c.wait()
        if r + 1 < PARENTS:
            for c in spots[r + 1][4]:
                c.start()
        from_first = lane >= shift
        outside = ((kz == 0) & (lane == shift)) | (
            (kz == nz // BS - 1) & (lane == lax.rem(shift + WIDE - 1, LANES))
        )

        def align(i, carry):
            for f in range(8):
                for y in range(3):
                    rows = slice(8 * y, 8 * y + 8)
                    value = jnp.where(
                        from_first, window[r, 0, f, i, rows], window[r, 1, f, i, rows]
                    )
                    value = jnp.where(outside, 1.0 if f == 0 else 0.0, value)
                    at = pl.multiple_of(f * PITCH + i * 24 + 8 * y, 8)
                    aligned[pl.ds(at, 8)] = value
            return carry

        lax.fori_loop(0, BS + 1, align, 0, unroll=True)

        def pair(number, carry):
            low_x, low_y = number // 2, number % 2
            plane_at = 8 * low_x - 1 + ix
            row_at = 8 * low_y - 1 + 8 * iy
            sums = None
            y_side = [zero, zero]
            z_side = [zero, zero]
            x_side = [zero, zero]
            held = None
            for i in range(SIDE):
                plane = jnp.clip(plane_at + i, 0, BS)
                sums = [zero, zero]
                z_low = [zero, zero]
                z_high = [zero, zero]
                inner = 0 < i < SIDE - 1
                for j in range(SIDE):
                    if not inner and not 0 < j < SIDE - 1:
                        continue
                    base = plane * 24 + jnp.clip(row_at + j, 0, 23)
                    value = aligned[pl.ds(base, 8, stride=PITCH), :]
                    if 0 < j < SIDE - 1:
                        moved = to_lane(value, 8 * (j - 1) - 1 - shift)
                        for c in range(2):
                            first = 8 * (j - 1) + 8 * c
                            sums[c] = jnp.where(lanes_from(lane, first, 8), moved, sums[c])
                            if inner:
                                z_low[c] = jnp.where(
                                    lanes_from(lane, first - 1, 1), moved, z_low[c]
                                )
                                z_high[c] = jnp.where(
                                    lanes_from(lane, first + 8, 1), moved, z_high[c]
                                )
                    else:
                        half, quarter = (i - 1) % 2, (i - 1) // 2
                        first = 64 * half + 16 * quarter + (8 if j else 0)
                        moved = to_lane(value, first - 1 - shift)
                        for c in range(2):
                            y_side[c] = jnp.where(
                                lanes_from(lane, first + 8 * c, 8), moved, y_side[c]
                            )
                for c in range(2):
                    child = 8 * r + 2 * number + c
                    if inner:
                        half, quarter = (i - 1) % 2, (i - 1) // 2
                        z_side[c] = put_z(lane, z_side[c], z_low[c], z_high[c], half, quarter, c)
                        if half:
                            out[child, 8 * quarter : 8 * quarter + 8] = jnp.where(
                                lane < 64, turned(held[c], -8 * c), turned(sums[c], 64 - 8 * c)
                            )
                    elif i:
                        x_side[c] = jnp.where(lane < 64, turned(sums[c], -8 * c), x_side[c])
                    else:
                        x_side[c] = turned(sums[c], 64 - 8 * c)
                held = sums
            for c in range(2):
                child = 8 * r + 2 * number + c
                out[child, X_ROWS] = x_side[c]
                out[child, Y_ROWS] = turned(y_side[c], -8 * c)
                out[child, Z_ROWS] = z_side[c]
            return carry

        lax.fori_loop(0, 4, pair, 0)

    for c in row_copies:
        c.wait()


def own_pieces(token, state, flags, owners):
    fields, _, ny, nz = state.shape
    return pl.pallas_call(
        own_kernel,
        out_shape=[
            jax.ShapeDtypeStruct((KIDS, ROWS, LANES), F32),
            jax.ShapeDtypeStruct((3 * PARENTS + KIDS,), jnp.int32),
        ]
        + [jax.ShapeDtypeStruct((fields + 1, ny, nz), F32)] * 2,
        in_specs=[SMEM, ANY, pl.BlockSpec(memory_space=pltpu.VMEM), SMEM],
        out_specs=[pl.BlockSpec(memory_space=pltpu.VMEM), SMEM]
        + [pl.BlockSpec(memory_space=pltpu.VMEM)] * 2,
        scratch_shapes=[
            pltpu.VMEM((PARENTS, 2, fields, BS + 1, 24, LANES), F32),
            pltpu.VMEM((fields * PITCH, LANES), F32),
            pltpu.SemaphoreType.DMA((PARENTS, 2, fields)),
            pltpu.SemaphoreType.DMA((2, 2)),
        ],
        compiler_params=pltpu.CompilerParams(vmem_limit_bytes=50 * MIB),
        cost_estimate=pl.CostEstimate(
            flops=10**7, bytes_accessed=20 * 10**6, transcendentals=0
        ),
        name="own_pieces",
    )(token, state, flags, owners)


def corner_kernel(col_even, col_odd, cor_even, cor_odd, ends, sems):
    nx = col_even.shape[1]
    nk = col_even.shape[2] // LANES
    copies = []
    for half, source in enumerate((col_even, col_odd)):
        for end in range(2):
            for k in range(nk):
                copies.append(
                    pltpu.make_async_copy(
                        source.at[:, pl.ds(end * (nx - 8), 8), pl.ds(k * LANES, LANES)],
                        ends.at[half, end, k],
                        sems.at[half, end, k],
                    )
                )
    for c in copies:
        c.start()
    for c in copies:
        c.wait()
    for number, ref in enumerate((cor_even, cor_odd)):
        end = 1 - parity("rows") if number == 0 else parity("rows")
        for half in range(2):
            for k in range(nk):
                cut = slice(k * LANES, (k + 1) * LANES)
                flat = flat_rows(ends.at[half, end, k])
                ref[half, 0:8, cut] = flat[pl.ds(7 * end, 8, stride=8), :]
                ref[half, 8:16, cut] = jnp.zeros((8, LANES), F32)
                ref[half, 8:9, cut] = flat[pl.ds(5 * 8 + 1 + 5 * end, 1), :]
                ref[half, 9:10, cut] = flat[pl.ds(8 * 8 + 7 * end, 1), :]


def pack_corners(col_even, col_odd):
    layers, _, nz = col_even.shape
    corner = jax.ShapeDtypeStruct((2, 16, nz), F32)
    return pl.pallas_call(
        corner_kernel,
        out_shape=[corner, corner],
        in_specs=[ANY] * 2,
        out_specs=[pl.BlockSpec(memory_space=pltpu.VMEM)] * 2,
        scratch_shapes=[
            pltpu.VMEM((2, 2, nz // LANES, layers, 8, LANES), F32),
            pltpu.SemaphoreType.DMA((2, 2, nz // LANES)),
        ],
        compiler_params=pltpu.CompilerParams(vmem_limit_bytes=8 * MIB),
        name="pack_corners",
    )(col_even, col_odd)


def finish_kernel(
    info, own, row_even, row_odd, col_even, col_odd, out, beside_x, beside_y, kid_sems, sems
):
    nk = row_even.shape[2] // LANES
    nx = col_even.shape[1]
    row_par, col_par = parity("rows"), parity("cols")
    waits = []
    for r in range(PARENTS):
        ix, iy, kz = info[3 * r], info[3 * r + 1], info[3 * r + 2]
        columns, shift = z_place(kz, nk)
        for t in range(2):

            def row_copy(source):
                return pltpu.make_async_copy(
                    source.at[pl.ds(0, 8), pl.ds(pl.multiple_of(iy * BS, BS), BS), columns[t]],
                    beside_x.at[r, t],
                    sems.at[r, t, 0],
                )

            def col_copy(source):
                return pltpu.make_async_copy(
                    source.at[pl.ds(0, 8), pl.ds(pl.multiple_of(ix * BS, BS), BS), columns[t]],
                    beside_y.at[r, t],
                    sems.at[r, t, 1],
                )

            @pl.when(ix != row_par)
            def _():
                row_copy(row_even).start()

            @pl.when(ix == row_par)
            def _():
                row_copy(row_odd).start()

            @pl.when(iy != col_par)
            def _():
                col_copy(col_even).start()

            @pl.when(iy == col_par)
            def _():
                col_copy(col_odd).start()

            waits += [row_copy(row_even), col_copy(col_even)]
    out[...] = jnp.zeros_like(out)
    kid_copies = [
        pltpu.make_async_copy(own.at[n], out.at[info[3 * PARENTS + n]], kid_sems.at[n])
        for n in range(KIDS)
    ]
    for c in kid_copies:
        c.start()
    for c in waits + kid_copies:
        c.wait()

    lane = lax.broadcasted_iota(jnp.int32, (8, LANES), 1)
    sub = lax.broadcasted_iota(jnp.int32, (8, LANES), 0)
    zero = jnp.zeros((8, LANES), F32)
    for r in range(PARENTS):
        ix, iy, kz = info[3 * r], info[3 * r + 1], info[3 * r + 2]
        _, shift = z_place(kz, nk)
        from_first = lane >= shift

        def cell(source, n):
            halves = [flat_rows(source.at[r, t])[pl.ds(n, 8, stride=BS), :] for t in range(2)]
            value = jnp.where(from_first, halves[0], halves[1])
            return jnp.where((sub == 0) & (value == 0.0), 1.0, value)

        first_kid = 3 * PARENTS + 8 * r
        here = (lane < 64) == (ix == 1)
        for b in range(2):
            sums = [zero, zero]
            for j in range(8):
                moved = to_lane(cell(beside_x, 8 * b + j), 8 * j - 1 - shift)
                for c in range(2):
                    sums[c] = jnp.where(lanes_from(lane, 8 * j + 8 * c, 8), moved, sums[c])
            for c in range(2):
                slot = info[first_kid + 4 * ix + 2 * b + c]
                value = to_lane(sums[c], 64 * (1 - ix) - 8 * c)
                out[slot, X_ROWS] = jnp.where(here, value, out[slot, X_ROWS])

        here = (lane // 8) % 2 == iy
        for a in range(2):
            sums = [zero, zero]
            for i in range(8):
                first = 64 * (i % 2) + 16 * (i // 2)
                moved = to_lane(cell(beside_y, 8 * a + i), first - 1 - shift)
                for c in range(2):
                    sums[c] = jnp.where(lanes_from(lane, first + 8 * c, 8), moved, sums[c])
            for c in range(2):
                slot = info[first_kid + 4 * a + 2 * iy + c]
                value = to_lane(sums[c], 8 * iy - 8 * c)
                out[slot, Y_ROWS] = jnp.where(here, value, out[slot, Y_ROWS])


def finish_pieces(info, own, rows_halo, cols_halo, count):
    return pl.pallas_call(
        finish_kernel,
        out_shape=jax.ShapeDtypeStruct((count * CAP, ROWS, LANES), F32),
        in_specs=[SMEM] + [ANY] * 5,
        out_specs=pl.BlockSpec(memory_space=pltpu.VMEM),
        scratch_shapes=[
            pltpu.VMEM((PARENTS, 2, 8, BS, LANES), F32),
            pltpu.VMEM((PARENTS, 2, 8, BS, LANES), F32),
            pltpu.SemaphoreType.DMA((KIDS,)),
            pltpu.SemaphoreType.DMA((PARENTS, 2, 2)),
        ],
        compiler_params=pltpu.CompilerParams(vmem_limit_bytes=8 * MIB),
        name="finish_pieces",
    )(info, own, *rows_halo, *cols_halo)


def spread_weights():
    spread = np.zeros((3, LANES, 512), np.float32)
    for half in range(2):
        for y in range(BS):
            for z in range(BS):
                at = half * 64 + y // 2 * 8 + z // 2
                to = half * 256 + y * BS + z
                spread[0, at, to] = 1.0
                spread[1, at, to] = 0.25 * (2 * (y % 2) - 1)
                spread[2, at, to] = 0.25 * (2 * (z % 2) - 1)
    return spread


def limited(left, right):
    return jnp.maximum(jnp.minimum(left, right), 0.0) + jnp.minimum(jnp.maximum(left, right), 0.0)


def halves_of(value):
    top = value.astype(BF16)
    return top, (value - top.astype(F32)).astype(BF16)


def prolong_kernel(weights, piece, out, staged):
    count = piece.shape[0]
    sub = lax.broadcasted_iota(jnp.int32, (8, LANES), 0)
    lane = lax.broadcasted_iota(jnp.int32, (8, LANES), 1)
    cells = sub < 5

    def slopes(s, carry):
        for q in range(4):
            one_set(s, q)
        return carry

    def one_set(s, q):
        here = piece[s, 8 * q : 8 * q + 8]
        after = piece[s, 8 * q + 8 : 8 * q + 16] if q < 3 else piece[s, X_ROWS]
        prior = piece[s, 8 * q - 8 : 8 * q] if q else piece[s, X_ROWS]
        rows, points = piece[s, Y_ROWS], piece[s, Z_ROWS]
        x_up = turned(jnp.where(lane < 64, after, here), 64) - here
        x_down = here - turned(jnp.where(lane < 64, here, prior), 64)
        y_up = jnp.where(lane % 64 >= 56, turned(rows, 48 - 16 * q), turned(here, -8)) - here
        y_down = here - jnp.where(lane % 64 < 8, turned(rows, -16 * q), turned(here, 8))
        z_up = jnp.where(lane % 8 == 7, turned(points, 6 - 2 * q), turned(here, -1)) - here
        z_down = here - jnp.where(lane % 8 == 0, turned(points, -2 * q), turned(here, 1))
        slope_x = jnp.where(cells, limited(x_up, x_down), jnp.where(sub == 5, x_up, 0.0))
        slope_y = jnp.where(cells, limited(y_up, y_down), jnp.where(sub == 6, y_up, 0.0))
        slope_z = jnp.where(cells, limited(z_up, z_down), jnp.where(sub == 7, z_up, 0.0))
        middle = here + jnp.where(cells, 0.0, 0.25 * (slope_x + slope_y + slope_z))
        at = pl.ds(pl.multiple_of(s * 32, 32) + 8 * q, 8)
        step = 0.25 * slope_x
        staged[0, at] = middle - step
        staged[1, at] = middle + step
        staged[2, at] = slope_y
        staged[3, at] = slope_z

    lax.fori_loop(0, count, slopes, 0)

    def dot(parts, matrix):
        halves = [halves_of(staged[n]) for n in parts]
        value = jnp.concatenate([h[0] for h in halves] + [h[1] for h in halves], axis=1)
        return jnp.dot(value, matrix, preferred_element_type=F32)

    tilt = dot((2, 3), weights[2 * LANES :])
    for p in range(2):
        fine = dot((p,), weights[0 : 2 * LANES]) + tilt
        for s in range(count):
            for i in range(8):
                x = 2 * i + p
                at = s * 32 + 8 * (i // 2)
                out[0, 0, s // 2, s % 2, :, x * 256 : (x + 1) * 256] = fine[
                    at : at + 8, 256 * (i % 2) : 256 * (i % 2) + 256
                ]


def prolong(received, count):
    group = 8
    weights = spread_weights()
    stacked = np.concatenate([weights[n] for n in (0, 0, 1, 2, 1, 2)])
    return pl.pallas_call(
        prolong_kernel,
        grid=(count * CAP // group,),
        out_shape=jax.ShapeDtypeStruct((1, 1, count, CAP, 8, BS**3), F32),
        in_specs=[
            pl.BlockSpec(stacked.shape, lambda g: (0, 0)),
            pl.BlockSpec((group, ROWS, LANES), lambda g: (g, 0, 0)),
        ],
        out_specs=pl.BlockSpec(
            (1, 1, group // CAP, CAP, 8, BS**3), lambda g: (0, 0, g, 0, 0, 0)
        ),
        scratch_shapes=[pltpu.VMEM((4, group * 32, LANES), F32)],
        compiler_params=pltpu.CompilerParams(vmem_limit_bytes=16 * MIB),
        name="prolong",
    )(jnp.asarray(stacked, BF16), received)


def on_device(state, flags, owners):
    rows, cols = lax.axis_size("rows"), lax.axis_size("cols")
    col_even, col_odd, token = pack(state)
    col_even = lax.ppermute(col_even, "cols", even_swap(cols))
    col_odd = lax.ppermute(col_odd, "cols", odd_swap(cols))
    own, info, row_even, row_odd = own_pieces(token, state, flags, owners)
    row_even = lax.ppermute(row_even, "rows", even_swap(rows))
    row_odd = lax.ppermute(row_odd, "rows", odd_swap(rows))
    cor_even, cor_odd = pack_corners(col_even, col_odd)
    cor_even = lax.ppermute(cor_even, "rows", even_swap(rows))
    cor_odd = lax.ppermute(cor_odd, "rows", odd_swap(rows))
    rows_halo, cols_halo = (row_even, row_odd), (col_even, col_odd)
    sent = finish_pieces(info, own, rows_halo, cols_halo, cols)
    sent, cor_even, cor_odd = lax.optimization_barrier((sent, cor_even, cor_odd))
    received = lax.all_to_all(
        sent.reshape((cols, CAP) + sent.shape[1:]), "cols", split_axis=0, concat_axis=0, tiled=True
    )
    faces_new = advance(state, rows_halo, cols_halo, (cor_even, cor_odd))
    arrivals = prolong(received.reshape(sent.shape), cols)
    return faces_new, arrivals


def solution(mesh):
    return jax.shard_map(
        on_device,
        mesh=mesh,
        in_specs=(
            P(None, "rows", "cols", None),
            P("rows", "cols", None),
            P(("rows", "cols"), None),
        ),
        out_specs=(P(None, "rows", "cols", None), P("rows", "cols", None, None, None, None)),
        check_vma=False,
    )
```

```python
import functools

import jax
import jax.numpy as jnp
import numpy as np
from jax import lax
from jax.experimental import pallas as pl
from jax.experimental.pallas import tpu as pltpu
from jax.sharding import PartitionSpec as P

F32 = jnp.float32
BF16 = jnp.bfloat16
BS = 16
CAP = 2
PARENTS = 2
KIDS = 16
LANES = 128
MIB = 1024 * 1024
ANY = pl.BlockSpec(memory_space=pl.ANY)
SMEM = pl.BlockSpec(memory_space=pltpu.SMEM)

courant = 0.3
SCALE = 0.25 * 0.5 * courant


def even_swap(count):
    return [(i, i ^ 1) for i in range(count)]


def odd_swap(count):
    return [p for i in range(1, count - 1, 2) for p in ((i, i + 1), (i + 1, i))]


def flat_rows(ref):
    rows = 1
    for n in ref.shape[:-1]:
        rows *= n
    return ref.reshape(rows, ref.shape[-1])


def parity(axis):
    return lax.rem(lax.axis_index(axis), 2)


def pack_kernel(state, col_even, col_odd, token, tiles, rims, sems, out_sems):
    nx, ny = state.shape[1], state.shape[2]
    nk = state.shape[3] // LANES

    def tile_in(side, k, f):
        return pltpu.make_async_copy(
            state.at[pl.ds(f, 2), :, pl.ds(side * (ny - 8), 8), pl.ds(k * LANES, LANES)],
            tiles.at[side, k, pl.ds(f, 2)],
            sems.at[side, k, f],
        )

    for k in range(nk):
        for side in range(2):
            for f in range(0, 8, 2):
                tile_in(side, k, f).start()
    high_in_even = parity("cols") == 0
    outs = []
    for k in range(nk):
        for side in range(2):
            for f in range(0, 8, 2):
                tile_in(side, k, f).wait()
        low_tile = flat_rows(tiles.at[0, k])
        high_tile = flat_rows(tiles.at[1, k])
        for layer in range(9):
            field = layer if layer < 8 else 6
            at_low = field * nx * 8 + (0 if layer < 8 else 1)
            at_high = field * nx * 8 + (7 if layer < 8 else 6)
            low = low_tile[pl.ds(at_low, nx, stride=8), :]
            high = high_tile[pl.ds(at_high, nx, stride=8), :]
            rims[0, k, layer] = jnp.where(high_in_even, high, low)
            rims[1, k, layer] = jnp.where(high_in_even, low, high)
        for number, ref in enumerate((col_even, col_odd)):
            c = pltpu.make_async_copy(
                rims.at[number, k],
                ref.at[:, :, pl.ds(k * LANES, LANES)],
                out_sems.at[number, k],
            )
            c.start()
            outs.append(c)
    token[0] = 0
    for c in outs:
        c.wait()


def pack(state):
    fields, nx, ny, nz = state.shape
    nk = nz // LANES
    col_shape = jax.ShapeDtypeStruct((fields + 1, nx, nz), F32)
    return pl.pallas_call(
        pack_kernel,
        out_shape=[col_shape, col_shape, jax.ShapeDtypeStruct((1,), jnp.int32)],
        in_specs=[ANY],
        out_specs=[ANY, ANY, SMEM],
        scratch_shapes=[
            pltpu.VMEM((2, nk, fields, nx, 8, LANES), F32),
            pltpu.VMEM((2, nk, fields + 1, nx, LANES), F32),
            pltpu.SemaphoreType.DMA((2, nk, fields)),
            pltpu.SemaphoreType.DMA((2, nk)),
        ],
        compiler_params=pltpu.CompilerParams(vmem_limit_bytes=50 * MIB),
        name="pack",
    )(state)


def lane_up(parts, lane):
    rolled = [pltpu.roll(p, LANES - 1, 1) for p in parts]
    rolled.append(jnp.zeros_like(parts[0]))
    return [jnp.where(lane == LANES - 1, rolled[k + 1], rolled[k]) for k in range(len(parts))]


def lane_down(parts, lane):
    rolled = [pltpu.roll(p, 1, 1) for p in parts]
    rolled = [jnp.zeros_like(parts[0])] + rolled
    return [jnp.where(lane == 0, rolled[k], rolled[k + 1]) for k in range(len(parts))]


def scaled_inverse(rho):
    guess = pl.reciprocal(rho, approx=True)
    guess = guess * (2.0 - rho * guess)
    guess = guess * (2.0 - rho * guess)
    return SCALE * guess


def advance_kernel(
    state, row_even, row_odd, col_even, col_odd, cor_even, cor_odd,
    out, dens, flds, rims, ends, rim_e, edge, prev, done, in_sems, halo_sems, out_sems,
):
    nx, ny, nz = state.shape[1:]
    nk = nz // LANES
    chunk = 4
    chunks = nx // chunk
    ahead = 3
    row_par, col_par = parity("rows"), parity("cols")

    def cut(k):
        return slice(k * LANES, (k + 1) * LANES)

    def chunk_in(c):
        at = pl.ds(c * chunk, chunk)
        to = pl.ds(1 + c * chunk, chunk)
        copies = [pltpu.make_async_copy(state.at[0, at], dens.at[to], in_sems.at[c, 0])]
        for f in range(6):
            copies.append(
                pltpu.make_async_copy(state.at[f + 2, at], flds.at[f, to], in_sems.at[c, f + 1])
            )
        return copies

    def rows_in(source, side):
        to = 0 if side == 0 else nx + 1
        copies = [
            pltpu.make_async_copy(source.at[0], dens.at[to], halo_sems.at[side, 0]),
            pltpu.make_async_copy(source.at[pl.ds(2, 6)], flds.at[:, to], halo_sems.at[side, 1]),
        ]
        if side == 1:
            copies.append(
                pltpu.make_async_copy(source.at[8], flds.at[3, nx + 2], halo_sems.at[side, 2])
            )
        return copies

    def cols_in(source, side):
        return [pltpu.make_async_copy(source, rims.at[side, :, pl.ds(8, nx)], halo_sems.at[side, 3])]

    corner_copies = [
        pltpu.make_async_copy(source, ends.at[n], halo_sems.at[n, 4])
        for n, source in enumerate((cor_even, cor_odd))
    ]
    for c in corner_copies:
        c.start()

    for side in range(2):
        @pl.when(row_par == side)
        def _():
            for c in rows_in(row_odd, side):
                c.start()

        @pl.when(row_par != side)
        def _():
            for c in rows_in(row_even, side):
                c.start()

        @pl.when(col_par == side)
        def _():
            for c in cols_in(col_odd, side):
                c.start()

        @pl.when(col_par != side)
        def _():
            for c in cols_in(col_even, side):
                c.start()

    for c in range(ahead):
        for copy in chunk_in(c):
            copy.start()

    for side in range(2):
        for c in rows_in(row_even, side) + cols_in(col_even, side):
            c.wait()

    for c in corner_copies:
        c.wait()
    for side in range(2):
        for end in range(2):
            row_swap = jnp.where(row_par == end, 1, 0)
            col_swap = jnp.where(col_par == side, 1, 0)
            at = 7 if end == 0 else nx + 8
            for f in range(8):
                rims[side, f, at : at + 1] = ends[row_swap, col_swap, f : f + 1]
            rims[side, 8, at : at + 1] = ends[row_swap, col_swap, 9:10]
            if end == 1:
                rims[side, 5, at + 1 : at + 2] = ends[row_swap, col_swap, 8:9]

    for at in (0, nx + 1):
        dens[at] = jnp.where(dens[at] > 0.0, dens[at], 1.0)

    span = rims.shape[2]
    rim_lane = lax.broadcasted_iota(jnp.int32, (span, LANES), 1)
    for side in range(2):
        face_z = [rims[side, 7, :, cut(k)] for k in range(nk)]
        face_z_up = lane_up(face_z, rim_lane)
        for k in range(nk):
            rho = rims[side, 0, :, cut(k)]
            inv = scaled_inverse(jnp.where(rho > 0.0, rho, 1.0))
            vel_x = rims[side, 2, :, cut(k)] * inv
            vel_y = rims[side, 3, :, cut(k)] * inv
            vel_z = rims[side, 4, :, cut(k)] * inv
            face_x = rims[side, 5, :, cut(k)]
            mag_x = face_x + pltpu.roll(face_x, span - 1, 0)
            mag_z = face_z[k] + face_z_up[k]
            mag_y = rims[side, 6, :, cut(k)]
            if side == 1:
                rim_e[3, 0, k] = mag_y
                mag_y = mag_y + rims[side, 8, :, cut(k)]
            rim_e[side, 0, k] = vel_y * mag_x - vel_x * mag_y
            rim_e[side, 1, k] = vel_z * mag_y - vel_y * mag_z
            if side == 0:
                rim_e[2, 0, k] = vel_x
                rim_e[2, 1, k] = vel_z

    prev[...] = jnp.zeros_like(prev)
    lane = lax.broadcasted_iota(jnp.int32, (8, LANES), 1)
    row = lax.broadcasted_iota(jnp.int32, (8, LANES), 0)
    zero = jnp.zeros((8, LANES), F32)
    nj = ny // 8

    def up_of(value):
        rolled = functools.cache(
            lambda k: pltpu.roll(value(k), LANES - 1, 1) if k < nk else zero
        )
        return lambda k: jnp.where(lane == LANES - 1, rolled(k + 1), rolled(k))

    def down_of(value):
        rolled = functools.cache(lambda k: pltpu.roll(value(k), 1, 1) if k >= 0 else zero)
        return lambda k: jnp.where(lane == 0, rolled(k - 1), rolled(k))

    def plane(p):
        at_rim = pl.ds(p + 7, 1)
        for k in range(nk):
            first = flds[4, p, 0:1, cut(k)]
            edge[0, k, 7:8] = rim_e[0, 0, k, at_rim] - rim_e[2, 0, k, at_rim] * first
            edge[1, k, 7:8] = rim_e[0, 1, k, at_rim] + rim_e[2, 1, k, at_rim] * first
            edge[0, k, ny + 8 : ny + 9] = rim_e[1, 0, k, at_rim]
            edge[1, k, ny + 8 : ny + 9] = rim_e[1, 1, k, at_rim]
        for j in range(nj):
            at = slice(8 * j, 8 * j + 8)
            to = slice(8 * j + 8, 8 * j + 16)
            face_z = functools.cache(lambda k: flds[5, p, at, cut(k)])
            face_z_up = up_of(face_z)
            for k in range(nk):
                inv = scaled_inverse(dens[p, at, cut(k)])
                vel_x = flds[0, p, at, cut(k)] * inv
                vel_y = flds[1, p, at, cut(k)] * inv
                vel_z = flds[2, p, at, cut(k)] * inv
                face_y = flds[4, p, at, cut(k)]
                mag_x = flds[3, p, at, cut(k)] + flds[3, p + 1, at, cut(k)]
                if j < nj - 1:
                    after = flds[4, p, 8 * j + 8 : 8 * j + 9, cut(k)]
                else:
                    after = rim_e[3, 0, k, at_rim]
                mag_y = face_y + jnp.where(row == 7, after, pltpu.roll(face_y, 7, 0))
                mag_z = face_z(k) + face_z_up(k)
                edge[0, k, to] = vel_y * mag_x - vel_x * mag_y
                edge[1, k, to] = vel_z * mag_y - vel_y * mag_z
                edge[2, k, to] = vel_x * mag_z - vel_z * mag_x
        before = jnp.maximum(p - 1, 0)
        for j in range(nj):
            at = slice(8 * j, 8 * j + 8)
            low, mid, high = (slice(8 * j + n, 8 * j + n + 8) for n in (7, 8, 9))
            elec_y = functools.cache(lambda k: edge[2, k, mid])
            x_sum = functools.cache(lambda k: edge[1, k, low] + edge[1, k, mid])
            x_diff = functools.cache(lambda k: edge[1, k, high] - edge[1, k, low])
            y_down, y_up = down_of(elec_y), up_of(elec_y)
            sum_down, sum_up = down_of(x_sum), up_of(x_sum)
            diff_down = down_of(x_diff)
            for k in range(nk):
                z_low = edge[0, k, low]
                below = y_down(k)
                turn = (edge[0, k, high] - z_low) - (y_up(k) - below)
                z_sum = z_low + edge[0, k, mid]
                y_sum = below + elec_y(k)
                done[0, p, at, cut(k)] = flds[3, p, at, cut(k)] - (prev[0, k, at] + turn)
                done[1, before, at, cut(k)] = prev[3, k, at] + z_sum
                done[2, before, at, cut(k)] = prev[4, k, at] - y_sum
                prev[3, k, at] = (flds[4, p, at, cut(k)] - prev[1, k, at]) - (
                    sum_up(k) - sum_down(k)
                )
                prev[4, k, at] = (flds[5, p, at, cut(k)] + prev[2, k, at]) + (
                    diff_down(k) + x_diff(k)
                )
                prev[0, k, at] = turn
                prev[1, k, at] = z_sum
                prev[2, k, at] = y_sum

    def chunk_out(c):
        return pltpu.make_async_copy(
            done.at[:, pl.ds(1 + c * chunk, chunk)],
            out.at[:, pl.ds(c * chunk, chunk)],
            out_sems.at[c],
        )

    def step(c, carry):
        for copy in chunk_in(c):
            copy.wait()

        @pl.when(c < chunks - ahead)
        def _():
            for copy in chunk_in(c + ahead):
                copy.start()

        for n in range(chunk):
            plane(c * chunk + n)

        @pl.when(c > 0)
        def _():
            chunk_out(c - 1).start()

        return carry

    lax.fori_loop(0, chunks, step, 0)
    plane(nx)
    plane(nx + 1)
    chunk_out(chunks - 1).start()
    for c in range(chunks):
        chunk_out(c).wait()


def advance(state, rows_halo, cols_halo, corners):
    nx, ny, nz = state.shape[1:]
    nk = nz // LANES
    return pl.pallas_call(
        advance_kernel,
        out_shape=jax.ShapeDtypeStruct((3, nx, ny, nz), F32),
        in_specs=[ANY] * 7,
        out_specs=ANY,
        scratch_shapes=[
            pltpu.VMEM((nx + 2, ny, nz), F32),
            pltpu.VMEM((6, nx + 3, ny, nz), F32),
            pltpu.VMEM((2, 9, nx + 16, nz), F32),
            pltpu.VMEM((2, 2, 16, nz), F32),
            pltpu.VMEM((4, 2, nk, nx + 16, LANES), F32),
            pltpu.VMEM((3, nk, ny + 16, LANES), F32),
            pltpu.VMEM((5, nk, ny, LANES), F32),
            pltpu.VMEM((3, nx + 2, ny, nz), F32),
            pltpu.SemaphoreType.DMA((nx // 4, 7)),
            pltpu.SemaphoreType.DMA((2, 6)),
            pltpu.SemaphoreType.DMA((nx // 4,)),
        ],
        compiler_params=pltpu.CompilerParams(vmem_limit_bytes=50 * MIB),
        cost_estimate=pl.CostEstimate(
            flops=60 * nx * ny * nz, bytes_accessed=40 * nx * ny * nz, transcendentals=0
        ),
        name="advance",
    )(state, *rows_halo, *cols_halo, *corners)


SIDE = BS // 2 + 2
WIDE = BS + 2


PITCH = (WIDE + 1) * 24


def z_place(kz, nk):
    begin = kz * BS - 1
    tile = (begin + LANES) // LANES - 1
    columns = [
        pl.ds(pl.multiple_of(jnp.clip(tile + t, 0, nk - 1) * LANES, LANES), LANES)
        for t in range(2)
    ]
    return columns, begin - tile * LANES


ROWS = 56
X_ROWS, Y_ROWS, Z_ROWS = slice(32, 40), slice(40, 48), slice(48, 56)


def turned(value, amount):
    return pltpu.roll(value, amount % LANES, 1) if amount % LANES else value


def to_lane(value, amount):
    return pltpu.roll(value, lax.rem(amount + 2 * LANES, LANES), 1)


def lanes_from(lane, first, count):
    first = first % LANES
    return (lane >= first) & (lane < first + count)


def put_z(lane, side, low, high, half, quarter, c):
    at = lane % 8
    here = (lane >= 64) if half else (lane < 64)
    low = turned(low, 64 * half + 2 * quarter + 1 - 8 * c)
    high = turned(high, 64 * half + 2 * quarter - 7 - 8 * c)
    side = jnp.where(here & (at == 2 * quarter), low, side)
    return jnp.where(here & (at == 2 * quarter + 1), high, side)


def own_kernel(
    token, state, flags, owners, out, info, row_even, row_odd,
    window, aligned, sems, row_sems,
):
    nx, ny, nz = state.shape[1:]
    nk = nz // LANES
    gx, gy, gz = flags.shape
    grid = (gy, gz)
    number = lax.broadcasted_iota(jnp.int32, grid, 0) * gz + lax.broadcasted_iota(
        jnp.int32, grid, 1
    )
    first = jnp.full(grid, gx * gy * gz - 1, jnp.int32)
    last = jnp.zeros(grid, jnp.int32)
    for x in range(gx):
        flagged = flags[x] == 1
        here = number + x * gy * gz
        first = jnp.minimum(first, jnp.where(flagged, here, gx * gy * gz - 1))
        last = jnp.maximum(last, jnp.where(flagged, here, 0))
    found = (
        jnp.min(first.astype(F32)).astype(jnp.int32),
        jnp.max(last.astype(F32)).astype(jnp.int32),
    )
    spots = []
    for r in range(PARENTS):
        ix, iy, kz = found[r] // (gy * gz), found[r] // gz % gy, found[r] % gz
        columns, shift = z_place(kz, nk)
        y_from = pl.multiple_of(8 * iy, 8)
        copies = []
        for f in range(8):
            for t in range(2):
                copies.append(
                    pltpu.make_async_copy(
                        state.at[f, pl.ds((BS - 1) * ix, BS + 1), pl.ds(y_from, 24), columns[t]],
                        window.at[r, t, f],
                        sems.at[r, t, f],
                    )
                )
        if r == 0:
            for c in copies:
                c.start()
        spots.append((ix, iy, kz, shift, copies))
        info[3 * r], info[3 * r + 1], info[3 * r + 2] = ix, iy, kz

    at_even = jnp.where(parity("rows") == 0, nx - 1, 0)
    at_odd = nx - 1 - at_even
    row_copies = []
    for number, (ref, at) in enumerate(((row_even, at_even), (row_odd, at_odd))):
        second = jnp.where(at == 0, 1, nx - 2)
        row_copies.append(
            pltpu.make_async_copy(state.at[:, at], ref.at[pl.ds(0, 8)], row_sems.at[number, 0])
        )
        row_copies.append(
            pltpu.make_async_copy(state.at[5, second], ref.at[8], row_sems.at[number, 1])
        )
    for c in row_copies:
        c.start()

    names = [owners[n, 0] for n in range(KIDS)]
    for n in range(KIDS):
        rank = jnp.int32(0)
        for m in range(n):
            rank = rank + jnp.where(names[m] == names[n], 1, 0)
        info[3 * PARENTS + n] = names[n] * CAP + rank

    lane = lax.broadcasted_iota(jnp.int32, (8, LANES), 1)
    zero = jnp.zeros((8, LANES), F32)
    for r in range(PARENTS):
        ix, iy, kz, shift, copies = spots[r]
        for c in copies:
            c.wait()
        if r + 1 < PARENTS:
            for c in spots[r + 1][4]:
                c.start()
        from_first = lane >= shift
        outside = ((kz == 0) & (lane == shift)) | (
            (kz == nz // BS - 1) & (lane == lax.rem(shift + WIDE - 1, LANES))
        )

        def align(i, carry):
            for f in range(8):
                for y in range(3):
                    rows = slice(8 * y, 8 * y + 8)
                    value = jnp.where(
                        from_first, window[r, 0, f, i, rows], window[r, 1, f, i, rows]
                    )
                    value = jnp.where(outside, 1.0 if f == 0 else 0.0, value)
                    at = pl.multiple_of(f * PITCH + i * 24 + 8 * y, 8)
                    aligned[pl.ds(at, 8)] = value
            return carry

        lax.fori_loop(0, BS + 1, align, 0, unroll=True)

        def pair(number, carry):
            low_x, low_y = number // 2, number % 2
            plane_at = 8 * low_x - 1 + ix
            row_at = 8 * low_y - 1 + 8 * iy
            sums = None
            y_side = [zero, zero]
            z_side = [zero, zero]
            x_side = [zero, zero]
            held = None
            for i in range(SIDE):
                plane = jnp.clip(plane_at + i, 0, BS)
                sums = [zero, zero]
                z_low = [zero, zero]
                z_high = [zero, zero]
                inner = 0 < i < SIDE - 1
                for j in range(SIDE):
                    if not inner and not 0 < j < SIDE - 1:
                        continue
                    base = plane * 24 + jnp.clip(row_at + j, 0, 23)
                    value = aligned[pl.ds(base, 8, stride=PITCH), :]
                    if 0 < j < SIDE - 1:
                        moved = to_lane(value, 8 * (j - 1) - 1 - shift)
                        for c in range(2):
                            first = 8 * (j - 1) + 8 * c
                            sums[c] = jnp.where(lanes_from(lane, first, 8), moved, sums[c])
                            if inner:
                                z_low[c] = jnp.where(
                                    lanes_from(lane, first - 1, 1), moved, z_low[c]
                                )
                                z_high[c] = jnp.where(
                                    lanes_from(lane, first + 8, 1), moved, z_high[c]
                                )
                    else:
                        half, quarter = (i - 1) % 2, (i - 1) // 2
                        first = 64 * half + 16 * quarter + (8 if j else 0)
                        moved = to_lane(value, first - 1 - shift)
                        for c in range(2):
                            y_side[c] = jnp.where(
                                lanes_from(lane, first + 8 * c, 8), moved, y_side[c]
                            )
                for c in range(2):
                    child = 8 * r + 2 * number + c
                    if inner:
                        half, quarter = (i - 1) % 2, (i - 1) // 2
                        z_side[c] = put_z(lane, z_side[c], z_low[c], z_high[c], half, quarter, c)
                        if half:
                            out[child, 8 * quarter : 8 * quarter + 8] = jnp.where(
                                lane < 64, turned(held[c], -8 * c), turned(sums[c], 64 - 8 * c)
                            )
                    elif i:
                        x_side[c] = jnp.where(lane < 64, turned(sums[c], -8 * c), x_side[c])
                    else:
                        x_side[c] = turned(sums[c], 64 - 8 * c)
                held = sums
            for c in range(2):
                child = 8 * r + 2 * number + c
                out[child, X_ROWS] = x_side[c]
                out[child, Y_ROWS] = turned(y_side[c], -8 * c)
                out[child, Z_ROWS] = z_side[c]
            return carry

        lax.fori_loop(0, 4, pair, 0)

    for c in row_copies:
        c.wait()


def own_pieces(token, state, flags, owners):
    fields, _, ny, nz = state.shape
    return pl.pallas_call(
        own_kernel,
        out_shape=[
            jax.ShapeDtypeStruct((KIDS, ROWS, LANES), F32),
            jax.ShapeDtypeStruct((3 * PARENTS + KIDS,), jnp.int32),
        ]
        + [jax.ShapeDtypeStruct((fields + 1, ny, nz), F32)] * 2,
        in_specs=[SMEM, ANY, pl.BlockSpec(memory_space=pltpu.VMEM), SMEM],
        out_specs=[pl.BlockSpec(memory_space=pltpu.VMEM), SMEM]
        + [pl.BlockSpec(memory_space=pltpu.VMEM)] * 2,
        scratch_shapes=[
            pltpu.VMEM((PARENTS, 2, fields, BS + 1, 24, LANES), F32),
            pltpu.VMEM((fields * PITCH, LANES), F32),
            pltpu.SemaphoreType.DMA((PARENTS, 2, fields)),
            pltpu.SemaphoreType.DMA((2, 2)),
        ],
        compiler_params=pltpu.CompilerParams(vmem_limit_bytes=50 * MIB),
        cost_estimate=pl.CostEstimate(
            flops=10**7, bytes_accessed=20 * 10**6, transcendentals=0
        ),
        name="own_pieces",
    )(token, state, flags, owners)


def corner_kernel(col_even, col_odd, cor_even, cor_odd, ends, sems):
    nx = col_even.shape[1]
    nk = col_even.shape[2] // LANES
    copies = []
    for half, source in enumerate((col_even, col_odd)):
        for end in range(2):
            for k in range(nk):
                copies.append(
                    pltpu.make_async_copy(
                        source.at[:, pl.ds(end * (nx - 8), 8), pl.ds(k * LANES, LANES)],
                        ends.at[half, end, k],
                        sems.at[half, end, k],
                    )
                )
    for c in copies:
        c.start()
    for c in copies:
        c.wait()
    for number, ref in enumerate((cor_even, cor_odd)):
        end = 1 - parity("rows") if number == 0 else parity("rows")
        for half in range(2):
            for k in range(nk):
                cut = slice(k * LANES, (k + 1) * LANES)
                flat = flat_rows(ends.at[half, end, k])
                ref[half, 0:8, cut] = flat[pl.ds(7 * end, 8, stride=8), :]
                ref[half, 8:16, cut] = jnp.zeros((8, LANES), F32)
                ref[half, 8:9, cut] = flat[pl.ds(5 * 8 + 1 + 5 * end, 1), :]
                ref[half, 9:10, cut] = flat[pl.ds(8 * 8 + 7 * end, 1), :]


def pack_corners(col_even, col_odd):
    layers, _, nz = col_even.shape
    corner = jax.ShapeDtypeStruct((2, 16, nz), F32)
    return pl.pallas_call(
        corner_kernel,
        out_shape=[corner, corner],
        in_specs=[ANY] * 2,
        out_specs=[pl.BlockSpec(memory_space=pltpu.VMEM)] * 2,
        scratch_shapes=[
            pltpu.VMEM((2, 2, nz // LANES, layers, 8, LANES), F32),
            pltpu.SemaphoreType.DMA((2, 2, nz // LANES)),
        ],
        compiler_params=pltpu.CompilerParams(vmem_limit_bytes=8 * MIB),
        name="pack_corners",
    )(col_even, col_odd)


def finish_kernel(
    info, own, row_even, row_odd, col_even, col_odd, out, beside_x, beside_y, kid_sems, sems
):
    nk = row_even.shape[2] // LANES
    nx = col_even.shape[1]
    row_par, col_par = parity("rows"), parity("cols")
    waits = []
    for r in range(PARENTS):
        ix, iy, kz = info[3 * r], info[3 * r + 1], info[3 * r + 2]
        columns, shift = z_place(kz, nk)
        for t in range(2):

            def row_copy(source):
                return pltpu.make_async_copy(
                    source.at[pl.ds(0, 8), pl.ds(pl.multiple_of(iy * BS, BS), BS), columns[t]],
                    beside_x.at[r, t],
                    sems.at[r, t, 0],
                )

            def col_copy(source):
                return pltpu.make_async_copy(
                    source.at[pl.ds(0, 8), pl.ds(pl.multiple_of(ix * BS, BS), BS), columns[t]],
                    beside_y.at[r, t],
                    sems.at[r, t, 1],
                )

            @pl.when(ix != row_par)
            def _():
                row_copy(row_even).start()

            @pl.when(ix == row_par)
            def _():
                row_copy(row_odd).start()

            @pl.when(iy != col_par)
            def _():
                col_copy(col_even).start()

            @pl.when(iy == col_par)
            def _():
                col_copy(col_odd).start()

            waits += [row_copy(row_even), col_copy(col_even)]
    out[...] = jnp.zeros_like(out)
    kid_copies = [
        pltpu.make_async_copy(own.at[n], out.at[info[3 * PARENTS + n]], kid_sems.at[n])
        for n in range(KIDS)
    ]
    for c in kid_copies:
        c.start()
    for c in waits + kid_copies:
        c.wait()

    lane = lax.broadcasted_iota(jnp.int32, (8, LANES), 1)
    sub = lax.broadcasted_iota(jnp.int32, (8, LANES), 0)
    zero = jnp.zeros((8, LANES), F32)
    for r in range(PARENTS):
        ix, iy, kz = info[3 * r], info[3 * r + 1], info[3 * r + 2]
        _, shift = z_place(kz, nk)
        from_first = lane >= shift

        def cell(source, n):
            halves = [flat_rows(source.at[r, t])[pl.ds(n, 8, stride=BS), :] for t in range(2)]
            value = jnp.where(from_first, halves[0], halves[1])
            return jnp.where((sub == 0) & (value == 0.0), 1.0, value)

        first_kid = 3 * PARENTS + 8 * r
        here = (lane < 64) == (ix == 1)
        for b in range(2):
            sums = [zero, zero]
            for j in range(8):
                moved = to_lane(cell(beside_x, 8 * b + j), 8 * j - 1 - shift)
                for c in range(2):
                    sums[c] = jnp.where(lanes_from(lane, 8 * j + 8 * c, 8), moved, sums[c])
            for c in range(2):
                slot = info[first_kid + 4 * ix + 2 * b + c]
                value = to_lane(sums[c], 64 * (1 - ix) - 8 * c)
                out[slot, X_ROWS] = jnp.where(here, value, out[slot, X_ROWS])

        here = (lane // 8) % 2 == iy
        for a in range(2):
            sums = [zero, zero]
            for i in range(8):
                first = 64 * (i % 2) + 16 * (i // 2)
                moved = to_lane(cell(beside_y, 8 * a + i), first - 1 - shift)
                for c in range(2):
                    sums[c] = jnp.where(lanes_from(lane, first + 8 * c, 8), moved, sums[c])
            for c in range(2):
                slot = info[first_kid + 4 * a + 2 * iy + c]
                value = to_lane(sums[c], 8 * iy - 8 * c)
                out[slot, Y_ROWS] = jnp.where(here, value, out[slot, Y_ROWS])


def finish_pieces(info, own, rows_halo, cols_halo, count):
    return pl.pallas_call(
        finish_kernel,
        out_shape=jax.ShapeDtypeStruct((count * CAP, ROWS, LANES), F32),
        in_specs=[SMEM] + [ANY] * 5,
        out_specs=pl.BlockSpec(memory_space=pltpu.VMEM),
        scratch_shapes=[
            pltpu.VMEM((PARENTS, 2, 8, BS, LANES), F32),
            pltpu.VMEM((PARENTS, 2, 8, BS, LANES), F32),
            pltpu.SemaphoreType.DMA((KIDS,)),
            pltpu.SemaphoreType.DMA((PARENTS, 2, 2)),
        ],
        compiler_params=pltpu.CompilerParams(vmem_limit_bytes=8 * MIB),
        name="finish_pieces",
    )(info, own, *rows_halo, *cols_halo)


def spread_weights():
    spread = np.zeros((3, 64, 256), np.float32)
    for y in range(BS):
        for z in range(BS):
            at = y // 2 * 8 + z // 2
            spread[0, at, y * BS + z] = 1.0
            spread[1, at, y * BS + z] = 0.25 * (2 * (y % 2) - 1)
            spread[2, at, y * BS + z] = 0.25 * (2 * (z % 2) - 1)
    return spread.reshape(192, 256)


def limited(left, right):
    return jnp.maximum(jnp.minimum(left, right), 0.0) + jnp.minimum(jnp.maximum(left, right), 0.0)


def halves_of(value):
    top = value.astype(BF16)
    return top, (value - top.astype(F32)).astype(BF16)


def prolong_kernel(blocks, piece, out, staged, weights):
    @pl.when(pl.program_id(0) == 0)
    def _():
        weights[...] = jnp.zeros_like(weights)
        for n, block in enumerate((0, 0, 1, 2, 1, 2)):
            for half in range(2):
                at = n * LANES + half * 64
                weights[at : at + 64, 256 * half : 256 * half + 256] = blocks[
                    64 * block : 64 * block + 64
                ]

    count = piece.shape[0]
    sub = lax.broadcasted_iota(jnp.int32, (8, LANES), 0)
    lane = lax.broadcasted_iota(jnp.int32, (8, LANES), 1)
    cells = sub < 5

    def slopes(s, carry):
        for q in range(4):
            one_set(s, q)
        return carry

    def one_set(s, q):
        here = piece[s, 8 * q : 8 * q + 8]
        after = piece[s, 8 * q + 8 : 8 * q + 16] if q < 3 else piece[s, X_ROWS]
        prior = piece[s, 8 * q - 8 : 8 * q] if q else piece[s, X_ROWS]
        rows, points = piece[s, Y_ROWS], piece[s, Z_ROWS]
        x_up = turned(jnp.where(lane < 64, after, here), 64) - here
        x_down = here - turned(jnp.where(lane < 64, here, prior), 64)
        y_up = jnp.where(lane % 64 >= 56, turned(rows, 48 - 16 * q), turned(here, -8)) - here
        y_down = here - jnp.where(lane % 64 < 8, turned(rows, -16 * q), turned(here, 8))
        z_up = jnp.where(lane % 8 == 7, turned(points, 6 - 2 * q), turned(here, -1)) - here
        z_down = here - jnp.where(lane % 8 == 0, turned(points, -2 * q), turned(here, 1))
        slope_x = jnp.where(cells, limited(x_up, x_down), jnp.where(sub == 5, x_up, 0.0))
        slope_y = jnp.where(cells, limited(y_up, y_down), jnp.where(sub == 6, y_up, 0.0))
        slope_z = jnp.where(cells, limited(z_up, z_down), jnp.where(sub == 7, z_up, 0.0))
        middle = here + jnp.where(cells, 0.0, 0.25 * (slope_x + slope_y + slope_z))
        at = pl.ds(pl.multiple_of(s * 32, 32) + 8 * q, 8)
        step = 0.25 * slope_x
        staged[0, at] = middle - step
        staged[1, at] = middle + step
        staged[2, at] = slope_y
        staged[3, at] = slope_z

    lax.fori_loop(0, count, slopes, 0, unroll=True)

    def dot(parts, matrix):
        halves = [halves_of(staged[n]) for n in parts]
        value = jnp.concatenate([h[0] for h in halves] + [h[1] for h in halves], axis=1)
        return jnp.dot(value, matrix, preferred_element_type=F32)

    tilt = dot((2, 3), weights[2 * LANES : 6 * LANES])
    for p in range(2):
        fine = dot((p,), weights[0 : 2 * LANES]) + tilt
        for s in range(count):
            for i in range(8):
                x = 2 * i + p
                at = s * 32 + 8 * (i // 2)
                out[0, 0, s // 2, s % 2, :, x * 256 : (x + 1) * 256] = fine[
                    at : at + 8, 256 * (i % 2) : 256 * (i % 2) + 256
                ]


def prolong(received, count):
    group = 8
    blocks = spread_weights()
    return pl.pallas_call(
        prolong_kernel,
        grid=(count * CAP // group,),
        out_shape=jax.ShapeDtypeStruct((1, 1, count, CAP, 8, BS**3), F32),
        in_specs=[
            pl.BlockSpec(blocks.shape, lambda g: (0, 0)),
            pl.BlockSpec((group, ROWS, LANES), lambda g: (g, 0, 0)),
        ],
        out_specs=pl.BlockSpec(
            (1, 1, group // CAP, CAP, 8, BS**3), lambda g: (0, 0, g, 0, 0, 0)
        ),
        scratch_shapes=[
            pltpu.VMEM((4, group * 32, LANES), F32),
            pltpu.VMEM((6 * LANES, 512), BF16),
        ],
        compiler_params=pltpu.CompilerParams(vmem_limit_bytes=16 * MIB),
        name="prolong",
    )(jnp.asarray(blocks, BF16), received)


def on_device(state, flags, owners):
    rows, cols = lax.axis_size("rows"), lax.axis_size("cols")
    col_even, col_odd, token = pack(state)
    col_even = lax.ppermute(col_even, "cols", even_swap(cols))
    col_odd = lax.ppermute(col_odd, "cols", odd_swap(cols))
    own, info, row_even, row_odd = own_pieces(token, state, flags, owners)
    row_even = lax.ppermute(row_even, "rows", even_swap(rows))
    row_odd = lax.ppermute(row_odd, "rows", odd_swap(rows))
    cor_even, cor_odd = pack_corners(col_even, col_odd)
    cor_even = lax.ppermute(cor_even, "rows", even_swap(rows))
    cor_odd = lax.ppermute(cor_odd, "rows", odd_swap(rows))
    rows_halo, cols_halo = (row_even, row_odd), (col_even, col_odd)
    sent = finish_pieces(info, own, rows_halo, cols_halo, cols)
    sent, cor_even, cor_odd = lax.optimization_barrier((sent, cor_even, cor_odd))
    received = lax.all_to_all(
        sent.reshape((cols, CAP) + sent.shape[1:]), "cols", split_axis=0, concat_axis=0, tiled=True
    )
    faces_new = advance(state, rows_halo, cols_halo, (cor_even, cor_odd))
    arrivals = prolong(received.reshape(sent.shape), cols)
    return faces_new, arrivals


def solution(mesh):
    return jax.shard_map(
        on_device,
        mesh=mesh,
        in_specs=(
            P(None, "rows", "cols", None),
            P("rows", "cols", None),
            P(("rows", "cols"), None),
        ),
        out_specs=(P(None, "rows", "cols", None), P("rows", "cols", None, None, None, None)),
        check_vma=False,
    )
```

```python
import functools

import jax
import jax.numpy as jnp
import numpy as np
from jax import lax
from jax.experimental import pallas as pl
from jax.experimental.pallas import tpu as pltpu
from jax.sharding import PartitionSpec as P

F32 = jnp.float32
BF16 = jnp.bfloat16
BS = 16
CAP = 2
PARENTS = 2
KIDS = 16
LANES = 128
MIB = 1024 * 1024
ANY = pl.BlockSpec(memory_space=pl.ANY)
SMEM = pl.BlockSpec(memory_space=pltpu.SMEM)

courant = 0.3
SCALE = 0.25 * 0.5 * courant


def even_swap(count):
    return [(i, i ^ 1) for i in range(count)]


def odd_swap(count):
    return [p for i in range(1, count - 1, 2) for p in ((i, i + 1), (i + 1, i))]


def flat_rows(ref):
    rows = 1
    for n in ref.shape[:-1]:
        rows *= n
    return ref.reshape(rows, ref.shape[-1])


def parity(axis):
    return lax.rem(lax.axis_index(axis), 2)


def pack_kernel(state, col_even, col_odd, token, tiles, rims, sems, out_sems):
    nx, ny = state.shape[1], state.shape[2]
    nk = state.shape[3] // LANES

    def tile_in(side, k, f):
        return pltpu.make_async_copy(
            state.at[pl.ds(f, 2), :, pl.ds(side * (ny - 8), 8), pl.ds(k * LANES, LANES)],
            tiles.at[side, k, pl.ds(f, 2)],
            sems.at[side, k, f],
        )

    for k in range(nk):
        for side in range(2):
            for f in range(0, 8, 2):
                tile_in(side, k, f).start()
    high_in_even = parity("cols") == 0
    outs = []
    for k in range(nk):
        for side in range(2):
            for f in range(0, 8, 2):
                tile_in(side, k, f).wait()
        low_tile = flat_rows(tiles.at[0, k])
        high_tile = flat_rows(tiles.at[1, k])
        for layer in range(9):
            field = layer if layer < 8 else 6
            at_low = field * nx * 8 + (0 if layer < 8 else 1)
            at_high = field * nx * 8 + (7 if layer < 8 else 6)
            low = low_tile[pl.ds(at_low, nx, stride=8), :]
            high = high_tile[pl.ds(at_high, nx, stride=8), :]
            rims[0, k, layer] = jnp.where(high_in_even, high, low)
            rims[1, k, layer] = jnp.where(high_in_even, low, high)
        for number, ref in enumerate((col_even, col_odd)):
            c = pltpu.make_async_copy(
                rims.at[number, k],
                ref.at[:, :, pl.ds(k * LANES, LANES)],
                out_sems.at[number, k],
            )
            c.start()
            outs.append(c)
    token[0] = 0
    for c in outs:
        c.wait()


def pack(state):
    fields, nx, ny, nz = state.shape
    nk = nz // LANES
    col_shape = jax.ShapeDtypeStruct((fields + 1, nx, nz), F32)
    return pl.pallas_call(
        pack_kernel,
        out_shape=[col_shape, col_shape, jax.ShapeDtypeStruct((1,), jnp.int32)],
        in_specs=[ANY],
        out_specs=[ANY, ANY, SMEM],
        scratch_shapes=[
            pltpu.VMEM((2, nk, fields, nx, 8, LANES), F32),
            pltpu.VMEM((2, nk, fields + 1, nx, LANES), F32),
            pltpu.SemaphoreType.DMA((2, nk, fields)),
            pltpu.SemaphoreType.DMA((2, nk)),
        ],
        compiler_params=pltpu.CompilerParams(vmem_limit_bytes=50 * MIB),
        name="pack",
    )(state)


def lane_up(parts, lane):
    rolled = [pltpu.roll(p, LANES - 1, 1) for p in parts]
    rolled.append(jnp.zeros_like(parts[0]))
    return [jnp.where(lane == LANES - 1, rolled[k + 1], rolled[k]) for k in range(len(parts))]


def lane_down(parts, lane):
    rolled = [pltpu.roll(p, 1, 1) for p in parts]
    rolled = [jnp.zeros_like(parts[0])] + rolled
    return [jnp.where(lane == 0, rolled[k], rolled[k + 1]) for k in range(len(parts))]


def scaled_inverse(rho):
    guess = pl.reciprocal(rho, approx=True)
    guess = guess * (2.0 - rho * guess)
    guess = guess * (2.0 - rho * guess)
    return SCALE * guess


def advance_kernel(
    state, row_even, row_odd, col_even, col_odd, cor_even, cor_odd,
    out, dens, flds, rims, ends, rim_e, edge, prev, done, in_sems, halo_sems, out_sems,
):
    nx, ny, nz = state.shape[1:]
    nk = nz // LANES
    chunk = 4
    chunks = nx // chunk
    ahead = 3
    row_par, col_par = parity("rows"), parity("cols")

    def cut(k):
        return slice(k * LANES, (k + 1) * LANES)

    def chunk_in(c):
        at = pl.ds(c * chunk, chunk)
        to = pl.ds(1 + c * chunk, chunk)
        copies = [pltpu.make_async_copy(state.at[0, at], dens.at[to], in_sems.at[c, 0])]
        for f in range(6):
            copies.append(
                pltpu.make_async_copy(state.at[f + 2, at], flds.at[f, to], in_sems.at[c, f + 1])
            )
        return copies

    def rows_in(source, side):
        to = 0 if side == 0 else nx + 1
        copies = [
            pltpu.make_async_copy(source.at[0], dens.at[to], halo_sems.at[side, 0]),
            pltpu.make_async_copy(source.at[pl.ds(2, 6)], flds.at[:, to], halo_sems.at[side, 1]),
        ]
        if side == 1:
            copies.append(
                pltpu.make_async_copy(source.at[8], flds.at[3, nx + 2], halo_sems.at[side, 2])
            )
        return copies

    def cols_in(source, side):
        return [pltpu.make_async_copy(source, rims.at[side, :, pl.ds(8, nx)], halo_sems.at[side, 3])]

    corner_copies = [
        pltpu.make_async_copy(source, ends.at[n], halo_sems.at[n, 4])
        for n, source in enumerate((cor_even, cor_odd))
    ]
    for c in corner_copies:
        c.start()

    for side in range(2):
        @pl.when(row_par == side)
        def _():
            for c in rows_in(row_odd, side):
                c.start()

        @pl.when(row_par != side)
        def _():
            for c in rows_in(row_even, side):
                c.start()

        @pl.when(col_par == side)
        def _():
            for c in cols_in(col_odd, side):
                c.start()

        @pl.when(col_par != side)
        def _():
            for c in cols_in(col_even, side):
                c.start()

    for c in range(ahead):
        for copy in chunk_in(c):
            copy.start()

    for side in range(2):
        for c in rows_in(row_even, side) + cols_in(col_even, side):
            c.wait()

    for c in corner_copies:
        c.wait()
    for side in range(2):
        for end in range(2):
            row_swap = jnp.where(row_par == end, 1, 0)
            col_swap = jnp.where(col_par == side, 1, 0)
            at = 7 if end == 0 else nx + 8
            for f in range(8):
                rims[side, f, at : at + 1] = ends[row_swap, col_swap, f : f + 1]
            rims[side, 8, at : at + 1] = ends[row_swap, col_swap, 9:10]
            if end == 1:
                rims[side, 5, at + 1 : at + 2] = ends[row_swap, col_swap, 8:9]

    for at in (0, nx + 1):
        dens[at] = jnp.where(dens[at] > 0.0, dens[at], 1.0)

    span = rims.shape[2]
    rim_lane = lax.broadcasted_iota(jnp.int32, (span, LANES), 1)
    for side in range(2):
        face_z = [rims[side, 7, :, cut(k)] for k in range(nk)]
        face_z_up = lane_up(face_z, rim_lane)
        for k in range(nk):
            rho = rims[side, 0, :, cut(k)]
            inv = scaled_inverse(jnp.where(rho > 0.0, rho, 1.0))
            vel_x = rims[side, 2, :, cut(k)] * inv
            vel_y = rims[side, 3, :, cut(k)] * inv
            vel_z = rims[side, 4, :, cut(k)] * inv
            face_x = rims[side, 5, :, cut(k)]
            mag_x = face_x + pltpu.roll(face_x, span - 1, 0)
            mag_z = face_z[k] + face_z_up[k]
            mag_y = rims[side, 6, :, cut(k)]
            if side == 1:
                rim_e[3, 0, k] = mag_y
                mag_y = mag_y + rims[side, 8, :, cut(k)]
            rim_e[side, 0, k] = vel_y * mag_x - vel_x * mag_y
            rim_e[side, 1, k] = vel_z * mag_y - vel_y * mag_z
            if side == 0:
                rim_e[2, 0, k] = vel_x
                rim_e[2, 1, k] = vel_z

    prev[...] = jnp.zeros_like(prev)
    lane = lax.broadcasted_iota(jnp.int32, (8, LANES), 1)
    row = lax.broadcasted_iota(jnp.int32, (8, LANES), 0)
    zero = jnp.zeros((8, LANES), F32)
    nj = ny // 8

    def up_of(value):
        rolled = functools.cache(
            lambda k: pltpu.roll(value(k), LANES - 1, 1) if k < nk else zero
        )
        return lambda k: jnp.where(lane == LANES - 1, rolled(k + 1), rolled(k))

    def down_of(value):
        rolled = functools.cache(lambda k: pltpu.roll(value(k), 1, 1) if k >= 0 else zero)
        return lambda k: jnp.where(lane == 0, rolled(k - 1), rolled(k))

    def plane(p):
        at_rim = pl.ds(p + 7, 1)
        for k in range(nk):
            first = flds[4, p, 0:1, cut(k)]
            edge[0, k, 7:8] = rim_e[0, 0, k, at_rim] - rim_e[2, 0, k, at_rim] * first
            edge[1, k, 7:8] = rim_e[0, 1, k, at_rim] + rim_e[2, 1, k, at_rim] * first
            edge[0, k, ny + 8 : ny + 9] = rim_e[1, 0, k, at_rim]
            edge[1, k, ny + 8 : ny + 9] = rim_e[1, 1, k, at_rim]
        for j in range(nj):
            at = slice(8 * j, 8 * j + 8)
            to = slice(8 * j + 8, 8 * j + 16)
            face_z = functools.cache(lambda k: flds[5, p, at, cut(k)])
            face_z_up = up_of(face_z)
            for k in range(nk):
                inv = scaled_inverse(dens[p, at, cut(k)])
                vel_x = flds[0, p, at, cut(k)] * inv
                vel_y = flds[1, p, at, cut(k)] * inv
                vel_z = flds[2, p, at, cut(k)] * inv
                face_y = flds[4, p, at, cut(k)]
                mag_x = flds[3, p, at, cut(k)] + flds[3, p + 1, at, cut(k)]
                if j < nj - 1:
                    after = flds[4, p, 8 * j + 8 : 8 * j + 9, cut(k)]
                else:
                    after = rim_e[3, 0, k, at_rim]
                mag_y = face_y + jnp.where(row == 7, after, pltpu.roll(face_y, 7, 0))
                mag_z = face_z(k) + face_z_up(k)
                edge[0, k, to] = vel_y * mag_x - vel_x * mag_y
                edge[1, k, to] = vel_z * mag_y - vel_y * mag_z
                edge[2, k, to] = vel_x * mag_z - vel_z * mag_x
        before = jnp.maximum(p - 1, 0)
        for j in range(nj):
            at = slice(8 * j, 8 * j + 8)
            low, mid, high = (slice(8 * j + n, 8 * j + n + 8) for n in (7, 8, 9))
            elec_y = functools.cache(lambda k: edge[2, k, mid])
            x_sum = functools.cache(lambda k: edge[1, k, low] + edge[1, k, mid])
            x_diff = functools.cache(lambda k: edge[1, k, high] - edge[1, k, low])
            y_down, y_up = down_of(elec_y), up_of(elec_y)
            sum_down, sum_up = down_of(x_sum), up_of(x_sum)
            diff_down = down_of(x_diff)
            for k in range(nk):
                z_low = edge[0, k, low]
                below = y_down(k)
                turn = (edge[0, k, high] - z_low) - (y_up(k) - below)
                z_sum = z_low + edge[0, k, mid]
                y_sum = below + elec_y(k)
                done[0, p, at, cut(k)] = flds[3, p, at, cut(k)] - (prev[0, k, at] + turn)
                done[1, before, at, cut(k)] = prev[3, k, at] + z_sum
                done[2, before, at, cut(k)] = prev[4, k, at] - y_sum
                prev[3, k, at] = (flds[4, p, at, cut(k)] - prev[1, k, at]) - (
                    sum_up(k) - sum_down(k)
                )
                prev[4, k, at] = (flds[5, p, at, cut(k)] + prev[2, k, at]) + (
                    diff_down(k) + x_diff(k)
                )
                prev[0, k, at] = turn
                prev[1, k, at] = z_sum
                prev[2, k, at] = y_sum

    def chunk_out(c):
        return pltpu.make_async_copy(
            done.at[:, pl.ds(1 + c * chunk, chunk)],
            out.at[:, pl.ds(c * chunk, chunk)],
            out_sems.at[c],
        )

    def step(c, carry):
        for copy in chunk_in(c):
            copy.wait()

        @pl.when(c < chunks - ahead)
        def _():
            for copy in chunk_in(c + ahead):
                copy.start()

        for n in range(chunk):
            plane(c * chunk + n)

        @pl.when(c > 0)
        def _():
            chunk_out(c - 1).start()

        return carry

    lax.fori_loop(0, chunks, step, 0)
    plane(nx)
    plane(nx + 1)
    chunk_out(chunks - 1).start()
    for c in range(chunks):
        chunk_out(c).wait()


def advance(state, rows_halo, cols_halo, corners):
    nx, ny, nz = state.shape[1:]
    nk = nz // LANES
    return pl.pallas_call(
        advance_kernel,
        out_shape=jax.ShapeDtypeStruct((3, nx, ny, nz), F32),
        in_specs=[ANY] * 7,
        out_specs=ANY,
        scratch_shapes=[
            pltpu.VMEM((nx + 2, ny, nz), F32),
            pltpu.VMEM((6, nx + 3, ny, nz), F32),
            pltpu.VMEM((2, 9, nx + 16, nz), F32),
            pltpu.VMEM((2, 2, 16, nz), F32),
            pltpu.VMEM((4, 2, nk, nx + 16, LANES), F32),
            pltpu.VMEM((3, nk, ny + 16, LANES), F32),
            pltpu.VMEM((5, nk, ny, LANES), F32),
            pltpu.VMEM((3, nx + 2, ny, nz), F32),
            pltpu.SemaphoreType.DMA((nx // 4, 7)),
            pltpu.SemaphoreType.DMA((2, 6)),
            pltpu.SemaphoreType.DMA((nx // 4,)),
        ],
        compiler_params=pltpu.CompilerParams(vmem_limit_bytes=50 * MIB),
        cost_estimate=pl.CostEstimate(
            flops=60 * nx * ny * nz, bytes_accessed=40 * nx * ny * nz, transcendentals=0
        ),
        name="advance",
    )(state, *rows_halo, *cols_halo, *corners)


SIDE = BS // 2 + 2
WIDE = BS + 2


PITCH = (WIDE + 1) * 24


def z_place(kz, nk):
    begin = kz * BS - 1
    tile = (begin + LANES) // LANES - 1
    columns = [
        pl.ds(pl.multiple_of(jnp.clip(tile + t, 0, nk - 1) * LANES, LANES), LANES)
        for t in range(2)
    ]
    return columns, begin - tile * LANES


ROWS = 56
X_ROWS, Y_ROWS, Z_ROWS = slice(32, 40), slice(40, 48), slice(48, 56)


def turned(value, amount):
    return pltpu.roll(value, amount % LANES, 1) if amount % LANES else value


def to_lane(value, amount):
    return pltpu.roll(value, lax.rem(amount + 2 * LANES, LANES), 1)


def lanes_from(lane, first, count):
    first = first % LANES
    return (lane >= first) & (lane < first + count)


def put_z(lane, side, low, high, half, quarter, c):
    at = lane % 8
    here = (lane >= 64) if half else (lane < 64)
    low = turned(low, 64 * half + 2 * quarter + 1 - 8 * c)
    high = turned(high, 64 * half + 2 * quarter - 7 - 8 * c)
    side = jnp.where(here & (at == 2 * quarter), low, side)
    return jnp.where(here & (at == 2 * quarter + 1), high, side)


def own_kernel(
    token, state, flags, owners, out, info, row_even, row_odd,
    window, aligned, sems, row_sems,
):
    nx, ny, nz = state.shape[1:]
    nk = nz // LANES
    gx, gy, gz = flags.shape
    grid = (gy, gz)
    number = lax.broadcasted_iota(jnp.int32, grid, 0) * gz + lax.broadcasted_iota(
        jnp.int32, grid, 1
    )
    first = jnp.full(grid, gx * gy * gz - 1, jnp.int32)
    last = jnp.zeros(grid, jnp.int32)
    for x in range(gx):
        flagged = flags[x] == 1
        here = number + x * gy * gz
        first = jnp.minimum(first, jnp.where(flagged, here, gx * gy * gz - 1))
        last = jnp.maximum(last, jnp.where(flagged, here, 0))
    found = (
        jnp.min(first.astype(F32)).astype(jnp.int32),
        jnp.max(last.astype(F32)).astype(jnp.int32),
    )
    spots = []
    for r in range(PARENTS):
        ix, iy, kz = found[r] // (gy * gz), found[r] // gz % gy, found[r] % gz
        columns, shift = z_place(kz, nk)
        y_from = pl.multiple_of(8 * iy, 8)
        copies = []
        for f in range(8):
            for t in range(2):
                copies.append(
                    pltpu.make_async_copy(
                        state.at[f, pl.ds((BS - 1) * ix, BS + 1), pl.ds(y_from, 24), columns[t]],
                        window.at[r, t, f],
                        sems.at[r, t, f],
                    )
                )
        if r == 0:
            for c in copies:
                c.start()
        spots.append((ix, iy, kz, shift, copies))
        info[3 * r], info[3 * r + 1], info[3 * r + 2] = ix, iy, kz

    at_even = jnp.where(parity("rows") == 0, nx - 1, 0)
    at_odd = nx - 1 - at_even
    row_copies = []
    for number, (ref, at) in enumerate(((row_even, at_even), (row_odd, at_odd))):
        second = jnp.where(at == 0, 1, nx - 2)
        row_copies.append(
            pltpu.make_async_copy(state.at[:, at], ref.at[pl.ds(0, 8)], row_sems.at[number, 0])
        )
        row_copies.append(
            pltpu.make_async_copy(state.at[5, second], ref.at[8], row_sems.at[number, 1])
        )
    for c in row_copies:
        c.start()

    names = [owners[n, 0] for n in range(KIDS)]
    for n in range(KIDS):
        rank = jnp.int32(0)
        for m in range(n):
            rank = rank + jnp.where(names[m] == names[n], 1, 0)
        info[3 * PARENTS + n] = names[n] * CAP + rank

    lane = lax.broadcasted_iota(jnp.int32, (8, LANES), 1)
    zero = jnp.zeros((8, LANES), F32)
    for r in range(PARENTS):
        ix, iy, kz, shift, copies = spots[r]
        for c in copies:
            c.wait()
        if r + 1 < PARENTS:
            for c in spots[r + 1][4]:
                c.start()
        from_first = lane >= shift
        outside = ((kz == 0) & (lane == shift)) | (
            (kz == nz // BS - 1) & (lane == lax.rem(shift + WIDE - 1, LANES))
        )

        def align(i, carry):
            for f in range(8):
                for y in range(3):
                    rows = slice(8 * y, 8 * y + 8)
                    value = jnp.where(
                        from_first, window[r, 0, f, i, rows], window[r, 1, f, i, rows]
                    )
                    value = jnp.where(outside, 1.0 if f == 0 else 0.0, value)
                    at = pl.multiple_of(f * PITCH + i * 24 + 8 * y, 8)
                    aligned[pl.ds(at, 8)] = value
            return carry

        lax.fori_loop(0, BS + 1, align, 0, unroll=True)

        def pair(number, carry):
            low_x, low_y = number // 2, number % 2
            plane_at = 8 * low_x - 1 + ix
            row_at = 8 * low_y - 1 + 8 * iy
            sums = None
            y_side = [zero, zero]
            z_side = [zero, zero]
            x_side = [zero, zero]
            held = None
            for i in range(SIDE):
                plane = jnp.clip(plane_at + i, 0, BS)
                sums = [zero, zero]
                z_low = [zero, zero]
                z_high = [zero, zero]
                inner = 0 < i < SIDE - 1
                for j in range(SIDE):
                    if not inner and not 0 < j < SIDE - 1:
                        continue
                    base = plane * 24 + jnp.clip(row_at + j, 0, 23)
                    value = aligned[pl.ds(base, 8, stride=PITCH), :]
                    if 0 < j < SIDE - 1:
                        moved = to_lane(value, 8 * (j - 1) - 1 - shift)
                        for c in range(2):
                            first = 8 * (j - 1) + 8 * c
                            sums[c] = jnp.where(lanes_from(lane, first, 8), moved, sums[c])
                            if inner:
                                z_low[c] = jnp.where(
                                    lanes_from(lane, first - 1, 1), moved, z_low[c]
                                )
                                z_high[c] = jnp.where(
                                    lanes_from(lane, first + 8, 1), moved, z_high[c]
                                )
                    else:
                        half, quarter = (i - 1) % 2, (i - 1) // 2
                        first = 64 * half + 16 * quarter + (8 if j else 0)
                        moved = to_lane(value, first - 1 - shift)
                        for c in range(2):
                            y_side[c] = jnp.where(
                                lanes_from(lane, first + 8 * c, 8), moved, y_side[c]
                            )
                for c in range(2):
                    child = 8 * r + 2 * number + c
                    if inner:
                        half, quarter = (i - 1) % 2, (i - 1) // 2
                        z_side[c] = put_z(lane, z_side[c], z_low[c], z_high[c], half, quarter, c)
                        if half:
                            out[child, 8 * quarter : 8 * quarter + 8] = jnp.where(
                                lane < 64, turned(held[c], -8 * c), turned(sums[c], 64 - 8 * c)
                            )
                    elif i:
                        x_side[c] = jnp.where(lane < 64, turned(sums[c], -8 * c), x_side[c])
                    else:
                        x_side[c] = turned(sums[c], 64 - 8 * c)
                held = sums
            for c in range(2):
                child = 8 * r + 2 * number + c
                out[child, X_ROWS] = x_side[c]
                out[child, Y_ROWS] = turned(y_side[c], -8 * c)
                out[child, Z_ROWS] = z_side[c]
            return carry

        lax.fori_loop(0, 4, pair, 0)

    for c in row_copies:
        c.wait()


def own_pieces(token, state, flags, owners):
    fields, _, ny, nz = state.shape
    return pl.pallas_call(
        own_kernel,
        out_shape=[
            jax.ShapeDtypeStruct((KIDS, ROWS, LANES), F32),
            jax.ShapeDtypeStruct((3 * PARENTS + KIDS,), jnp.int32),
        ]
        + [jax.ShapeDtypeStruct((fields + 1, ny, nz), F32)] * 2,
        in_specs=[SMEM, ANY, pl.BlockSpec(memory_space=pltpu.VMEM), SMEM],
        out_specs=[pl.BlockSpec(memory_space=pltpu.VMEM), SMEM]
        + [pl.BlockSpec(memory_space=pltpu.VMEM)] * 2,
        scratch_shapes=[
            pltpu.VMEM((PARENTS, 2, fields, BS + 1, 24, LANES), F32),
            pltpu.VMEM((fields * PITCH, LANES), F32),
            pltpu.SemaphoreType.DMA((PARENTS, 2, fields)),
            pltpu.SemaphoreType.DMA((2, 2)),
        ],
        compiler_params=pltpu.CompilerParams(vmem_limit_bytes=50 * MIB),
        cost_estimate=pl.CostEstimate(
            flops=10**7, bytes_accessed=20 * 10**6, transcendentals=0
        ),
        name="own_pieces",
    )(token, state, flags, owners)


def corner_kernel(col_even, col_odd, cor_even, cor_odd, ends, sems):
    nx = col_even.shape[1]
    nk = col_even.shape[2] // LANES
    copies = []
    for half, source in enumerate((col_even, col_odd)):
        for end in range(2):
            for k in range(nk):
                copies.append(
                    pltpu.make_async_copy(
                        source.at[:, pl.ds(end * (nx - 8), 8), pl.ds(k * LANES, LANES)],
                        ends.at[half, end, k],
                        sems.at[half, end, k],
                    )
                )
    for c in copies:
        c.start()
    for c in copies:
        c.wait()
    for number, ref in enumerate((cor_even, cor_odd)):
        end = 1 - parity("rows") if number == 0 else parity("rows")
        for half in range(2):
            for k in range(nk):
                cut = slice(k * LANES, (k + 1) * LANES)
                flat = flat_rows(ends.at[half, end, k])
                ref[half, 0:8, cut] = flat[pl.ds(7 * end, 8, stride=8), :]
                ref[half, 8:16, cut] = jnp.zeros((8, LANES), F32)
                ref[half, 8:9, cut] = flat[pl.ds(5 * 8 + 1 + 5 * end, 1), :]
                ref[half, 9:10, cut] = flat[pl.ds(8 * 8 + 7 * end, 1), :]


def pack_corners(col_even, col_odd):
    layers, _, nz = col_even.shape
    corner = jax.ShapeDtypeStruct((2, 16, nz), F32)
    return pl.pallas_call(
        corner_kernel,
        out_shape=[corner, corner],
        in_specs=[ANY] * 2,
        out_specs=[pl.BlockSpec(memory_space=pltpu.VMEM)] * 2,
        scratch_shapes=[
            pltpu.VMEM((2, 2, nz // LANES, layers, 8, LANES), F32),
            pltpu.SemaphoreType.DMA((2, 2, nz // LANES)),
        ],
        compiler_params=pltpu.CompilerParams(vmem_limit_bytes=8 * MIB),
        name="pack_corners",
    )(col_even, col_odd)


def finish_kernel(
    info, own, row_even, row_odd, col_even, col_odd, out, beside_x, beside_y, kid_sems, sems
):
    nk = row_even.shape[2] // LANES
    nx = col_even.shape[1]
    row_par, col_par = parity("rows"), parity("cols")
    waits = []
    for r in range(PARENTS):
        ix, iy, kz = info[3 * r], info[3 * r + 1], info[3 * r + 2]
        columns, shift = z_place(kz, nk)
        for t in range(2):

            def row_copy(source):
                return pltpu.make_async_copy(
                    source.at[pl.ds(0, 8), pl.ds(pl.multiple_of(iy * BS, BS), BS), columns[t]],
                    beside_x.at[r, t],
                    sems.at[r, t, 0],
                )

            def col_copy(source):
                return pltpu.make_async_copy(
                    source.at[pl.ds(0, 8), pl.ds(pl.multiple_of(ix * BS, BS), BS), columns[t]],
                    beside_y.at[r, t],
                    sems.at[r, t, 1],
                )

            @pl.when(ix != row_par)
            def _():
                row_copy(row_even).start()

            @pl.when(ix == row_par)
            def _():
                row_copy(row_odd).start()

            @pl.when(iy != col_par)
            def _():
                col_copy(col_even).start()

            @pl.when(iy == col_par)
            def _():
                col_copy(col_odd).start()

            waits += [row_copy(row_even), col_copy(col_even)]
    out[...] = jnp.zeros_like(out)
    kid_copies = [
        pltpu.make_async_copy(own.at[n], out.at[info[3 * PARENTS + n]], kid_sems.at[n])
        for n in range(KIDS)
    ]
    for c in kid_copies:
        c.start()
    for c in waits + kid_copies:
        c.wait()

    lane = lax.broadcasted_iota(jnp.int32, (8, LANES), 1)
    sub = lax.broadcasted_iota(jnp.int32, (8, LANES), 0)
    zero = jnp.zeros((8, LANES), F32)
    for r in range(PARENTS):
        ix, iy, kz = info[3 * r], info[3 * r + 1], info[3 * r + 2]
        _, shift = z_place(kz, nk)
        from_first = lane >= shift

        def cell(source, n):
            halves = [flat_rows(source.at[r, t])[pl.ds(n, 8, stride=BS), :] for t in range(2)]
            value = jnp.where(from_first, halves[0], halves[1])
            return jnp.where((sub == 0) & (value == 0.0), 1.0, value)

        first_kid = 3 * PARENTS + 8 * r
        here = (lane < 64) == (ix == 1)
        for b in range(2):
            sums = [zero, zero]
            for j in range(8):
                moved = to_lane(cell(beside_x, 8 * b + j), 8 * j - 1 - shift)
                for c in range(2):
                    sums[c] = jnp.where(lanes_from(lane, 8 * j + 8 * c, 8), moved, sums[c])
            for c in range(2):
                slot = info[first_kid + 4 * ix + 2 * b + c]
                value = to_lane(sums[c], 64 * (1 - ix) - 8 * c)
                out[slot, X_ROWS] = jnp.where(here, value, out[slot, X_ROWS])

        here = (lane // 8) % 2 == iy
        for a in range(2):
            sums = [zero, zero]
            for i in range(8):
                first = 64 * (i % 2) + 16 * (i // 2)
                moved = to_lane(cell(beside_y, 8 * a + i), first - 1 - shift)
                for c in range(2):
                    sums[c] = jnp.where(lanes_from(lane, first + 8 * c, 8), moved, sums[c])
            for c in range(2):
                slot = info[first_kid + 4 * a + 2 * iy + c]
                value = to_lane(sums[c], 8 * iy - 8 * c)
                out[slot, Y_ROWS] = jnp.where(here, value, out[slot, Y_ROWS])


def finish_pieces(info, own, rows_halo, cols_halo, count):
    return pl.pallas_call(
        finish_kernel,
        out_shape=jax.ShapeDtypeStruct((count * CAP, ROWS, LANES), F32),
        in_specs=[SMEM] + [ANY] * 5,
        out_specs=pl.BlockSpec(memory_space=pltpu.VMEM),
        scratch_shapes=[
            pltpu.VMEM((PARENTS, 2, 8, BS, LANES), F32),
            pltpu.VMEM((PARENTS, 2, 8, BS, LANES), F32),
            pltpu.SemaphoreType.DMA((KIDS,)),
            pltpu.SemaphoreType.DMA((PARENTS, 2, 2)),
        ],
        compiler_params=pltpu.CompilerParams(vmem_limit_bytes=8 * MIB),
        name="finish_pieces",
    )(info, own, *rows_halo, *cols_halo)


def spread_weights():
    spread = np.zeros((3, 64, 256), np.float32)
    for y in range(BS):
        for z in range(BS):
            at = y // 2 * 8 + z // 2
            spread[0, at, y * BS + z] = 1.0
            spread[1, at, y * BS + z] = 0.25 * (2 * (y % 2) - 1)
            spread[2, at, y * BS + z] = 0.25 * (2 * (z % 2) - 1)
    return spread.reshape(192, 256)


def limited(left, right):
    return jnp.maximum(jnp.minimum(left, right), 0.0) + jnp.minimum(jnp.maximum(left, right), 0.0)


def halves_of(value):
    top = value.astype(BF16)
    return top, (value - top.astype(F32)).astype(BF16)


def prolong_kernel(blocks, piece, out, staged, weights):
    @pl.when(pl.program_id(0) == 0)
    def _():
        weights[...] = jnp.zeros_like(weights)
        for n, block in enumerate((0, 0, 1, 2, 1, 2)):
            for half in range(2):
                at = n * LANES + half * 64
                weights[at : at + 64, 256 * half : 256 * half + 256] = blocks[
                    64 * block : 64 * block + 64
                ]

    count = piece.shape[0]
    sub = lax.broadcasted_iota(jnp.int32, (8, LANES), 0)
    lane = lax.broadcasted_iota(jnp.int32, (8, LANES), 1)
    cells = sub < 5

    def slopes(s, carry):
        for q in range(4):
            one_set(s, q)
        return carry

    def one_set(s, q):
        here = piece[s, 8 * q : 8 * q + 8]
        after = piece[s, 8 * q + 8 : 8 * q + 16] if q < 3 else piece[s, X_ROWS]
        prior = piece[s, 8 * q - 8 : 8 * q] if q else piece[s, X_ROWS]
        rows, points = piece[s, Y_ROWS], piece[s, Z_ROWS]
        x_up = turned(jnp.where(lane < 64, after, here), 64) - here
        x_down = here - turned(jnp.where(lane < 64, here, prior), 64)
        y_up = jnp.where(lane % 64 >= 56, turned(rows, 48 - 16 * q), turned(here, -8)) - here
        y_down = here - jnp.where(lane % 64 < 8, turned(rows, -16 * q), turned(here, 8))
        z_up = jnp.where(lane % 8 == 7, turned(points, 6 - 2 * q), turned(here, -1)) - here
        z_down = here - jnp.where(lane % 8 == 0, turned(points, -2 * q), turned(here, 1))
        slope_x = jnp.where(cells, limited(x_up, x_down), jnp.where(sub == 5, x_up, 0.0))
        slope_y = jnp.where(cells, limited(y_up, y_down), jnp.where(sub == 6, y_up, 0.0))
        slope_z = jnp.where(cells, limited(z_up, z_down), jnp.where(sub == 7, z_up, 0.0))
        middle = here + jnp.where(cells, 0.0, 0.25 * (slope_x + slope_y + slope_z))
        at = pl.ds(pl.multiple_of(s * 32, 32) + 8 * q, 8)
        step = 0.25 * slope_x
        staged[0, at] = middle - step
        staged[1, at] = middle + step
        staged[2, at] = slope_y
        staged[3, at] = slope_z

    lax.fori_loop(0, count, slopes, 0, unroll=True)

    def dot(parts, matrix):
        halves = [halves_of(staged[n]) for n in parts]
        value = jnp.concatenate([h[0] for h in halves] + [h[1] for h in halves], axis=1)
        return jnp.dot(value, matrix, preferred_element_type=F32)

    tilt = dot((2, 3), weights[2 * LANES : 6 * LANES])
    for p in range(2):
        fine = dot((p,), weights[0 : 2 * LANES]) + tilt
        for s in range(count):
            for i in range(8):
                x = 2 * i + p
                at = s * 32 + 8 * (i // 2)
                out[0, 0, s // 2, s % 2, :, x * 256 : (x + 1) * 256] = fine[
                    at : at + 8, 256 * (i % 2) : 256 * (i % 2) + 256
                ]


def prolong(received, count):
    group = 16
    blocks = spread_weights()
    return pl.pallas_call(
        prolong_kernel,
        grid=(count * CAP // group,),
        out_shape=jax.ShapeDtypeStruct((1, 1, count, CAP, 8, BS**3), F32),
        in_specs=[
            pl.BlockSpec(blocks.shape, lambda g: (0, 0)),
            pl.BlockSpec((group, ROWS, LANES), lambda g: (g, 0, 0)),
        ],
        out_specs=pl.BlockSpec(
            (1, 1, group // CAP, CAP, 8, BS**3), lambda g: (0, 0, g, 0, 0, 0)
        ),
        scratch_shapes=[
            pltpu.VMEM((4, group * 32, LANES), F32),
            pltpu.VMEM((6 * LANES, 512), BF16),
        ],
        compiler_params=pltpu.CompilerParams(vmem_limit_bytes=16 * MIB),
        name="prolong",
    )(jnp.asarray(blocks, BF16), received)


def on_device(state, flags, owners):
    rows, cols = lax.axis_size("rows"), lax.axis_size("cols")
    col_even, col_odd, token = pack(state)
    col_even = lax.ppermute(col_even, "cols", even_swap(cols))
    col_odd = lax.ppermute(col_odd, "cols", odd_swap(cols))
    own, info, row_even, row_odd = own_pieces(token, state, flags, owners)
    row_even = lax.ppermute(row_even, "rows", even_swap(rows))
    row_odd = lax.ppermute(row_odd, "rows", odd_swap(rows))
    cor_even, cor_odd = pack_corners(col_even, col_odd)
    cor_even = lax.ppermute(cor_even, "rows", even_swap(rows))
    cor_odd = lax.ppermute(cor_odd, "rows", odd_swap(rows))
    rows_halo, cols_halo = (row_even, row_odd), (col_even, col_odd)
    sent = finish_pieces(info, own, rows_halo, cols_halo, cols)
    sent, cor_even, cor_odd = lax.optimization_barrier((sent, cor_even, cor_odd))
    received = lax.all_to_all(
        sent.reshape((cols, CAP) + sent.shape[1:]), "cols", split_axis=0, concat_axis=0, tiled=True
    )
    faces_new = advance(state, rows_halo, cols_halo, (cor_even, cor_odd))
    arrivals = prolong(received.reshape(sent.shape), cols)
    return faces_new, arrivals


def solution(mesh):
    return jax.shard_map(
        on_device,
        mesh=mesh,
        in_specs=(
            P(None, "rows", "cols", None),
            P("rows", "cols", None),
            P(("rows", "cols"), None),
        ),
        out_specs=(P(None, "rows", "cols", None), P("rows", "cols", None, None, None, None)),
        check_vma=False,
    )
```
